128 devices in a mesh: row: 16 (over x, y), col: 8 (over z, core).
Axes of the slice: x: 4, y: 4, z: 4, core: 2. Of those that a mesh axis runs over, the one named last changes fastest.
Arguments:
- tokens: bfloat16 [1024, 12288], P('col', 'row'), may hold values from -6 to 6
- grad_out: bfloat16 [1024, 12288], P('col', 'row'), may hold values from -6 to 6
- up_weight: bfloat16 [12288, 24576], P('row', 'col'), may hold values from -0.0546875 to 0.0546875
- down_weight: bfloat16 [24576, 12288], P('col', 'row'), may hold values from -0.0390625 to 0.0390625
- up_bias: float32 [24576], P('col'), may hold values from -4 to 4
- relu_bits: int32 [1024, 1536], P('row', 'col'), may hold values from 0 to 65535
- drop_bits: int32 [1024, 1536], P('row', 'col'), may hold values from 0 to 65535, as said below
Outputs:
- grad_tokens: bfloat16 [1024, 12288], P('col', 'row')
- grad_up: bfloat16 [12288, 24576], P('row', 'col')
- grad_down: bfloat16 [24576, 12288], P('col', 'row')
- grad_bias: float32 [24576], P('col')
The draws below stay inside these ranges and needn't reach their ends.
Inputs may be any that keep to these rules, and one draw needn't show every extreme that they name: `relu_bits`: bit k of word j of token t is the saved ReLU mask of hidden unit 16 j + k. `drop_bits`: bit k of word j of token t is 1 where dropout kept hidden unit 16 j + k of token t.
All inputs are finite; a program needn't handle non-finite values.
Results may differ from the reference program's by a relative error of at most 0.03.
Values may be sent and summed in bfloat16 or wider, within the bound.
A program may use at most 128 MiB of HBM per device.

```python
import math
import jax
import jax.numpy as jnp
from jax import lax

D = 12288
FF = 24576
TOKENS = 1024
N_ROW = 16


def draw_drop_bits(key, part):
    key = jax.random.fold_in(key, 7)
    kept = (jax.random.randint(key, (TOKENS, FF // 16, 16), 0, 10) > 0).astype(jnp.int32)
    powers = jnp.left_shift(jnp.ones((16,), jnp.int32), jnp.arange(16, dtype=jnp.int32))
    return jnp.sum(kept * powers[None, None, :], axis=-1).astype(jnp.int32)


def plant(result, stream_key, least, largest):
    shape = result.shape
    index_at = [jax.random.randint(jax.random.fold_in(stream_key, axis), (), 0, shape[axis]) for axis in range(len(shape))]
    result = result.at[tuple(index_at)].set(least)
    longest = shape.index(max(shape))
    index_at[longest] = (index_at[longest] + 1) % shape[longest]
    return result.at[tuple(index_at)].set(largest)


def block_levels(rng, shape, pieces, low, top_value):
    def one(axis_at, shards_of):
        draws = jax.random.uniform(jax.random.fold_in(jax.random.fold_in(rng, 6), axis_at), (shards_of,), jnp.float32, low / len(pieces), top_value / len(pieces))
        return jnp.repeat(jnp.exp(draws), shape[axis_at] // shards_of).reshape((-1,) + (1,) * (len(shape) - axis_at - 1))

    loudness = one(*pieces[0])
    for cut in pieces[1:]:
        loudness = loudness * one(*cut)
    return loudness


def normal_values(key, extent, scale, most, split=(), kind=jnp.bfloat16):
    factor_of = block_levels(key, extent, split, -0.22, 0.18) if split else 1.0
    drawn = jax.random.normal(key, extent, jnp.float32) * scale * factor_of
    return jnp.minimum(jnp.maximum(drawn, -most), most).astype(kind)


def setup_inputs(seed: int = 0) -> dict:
    seeds = jax.random.split(jax.random.key(seed), 8)
    return {
        "tokens": normal_values(seeds[0], (TOKENS, D), 1.0, 6.0, ((0, 8), (1, 16))),
        "grad_out": normal_values(seeds[1], (TOKENS, D), 1.0, 6.0, ((0, 8), (1, 16))),
        "up_weight": normal_values(seeds[2], (D, FF), D ** -0.5, 0.0546875, ((0, 16), (1, 8))),
        "down_weight": normal_values(seeds[3], (FF, D), FF ** -0.5, 0.0390625, ((0, 8), (1, 16))),
        "up_bias": normal_values(seeds[4], (FF,), 1.0, 4.0, ((0, 8),), jnp.float32),
        "relu_bits": plant(jax.random.randint(seeds[5], (TOKENS, FF // 16), 0, 65536), jax.random.fold_in(seeds[5], 1), 0, 65535).astype(jnp.int32),
        "drop_bits": draw_drop_bits(jax.random.fold_in(seeds[7], 71), 0),
    }


keep_rate = 0.9

def unpack(words):
    shifts = jnp.arange(16, dtype=jnp.int32)
    bits = jnp.right_shift(words[:, :, None], shifts[None, None, :]) & 1
    return bits.reshape(words.shape[0], words.shape[1] * 16).astype(jnp.float32)

def blocked_sum(left_blocks, right_blocks):

    def step(total, pair):
        part = jnp.dot(pair[0], pair[1], preferred_element_type=jnp.float32)
        part = lax.optimization_barrier(part.astype(jnp.bfloat16))
        return (total + part.astype(jnp.float32), None)
    start = jnp.zeros((left_blocks.shape[1], right_blocks.shape[2]), jnp.float32)
    total, unused = lax.scan(step, start, (left_blocks, right_blocks))
    return total

def reference(tokens, grad_out, up_weight, down_weight, up_bias, relu_bits, drop_bits):
    width = D // N_ROW
    keep = unpack(relu_bits) * unpack(drop_bits) * (1.0 / keep_rate)
    token_blocks = tokens.reshape(TOKENS, N_ROW, width).transpose(1, 0, 2)
    grad_blocks = grad_out.reshape(TOKENS, N_ROW, width).transpose(1, 0, 2)
    up_blocks = up_weight.reshape(N_ROW, width, FF)
    down_blocks = down_weight.reshape(FF, N_ROW, width).transpose(1, 2, 0)
    pre = blocked_sum(token_blocks, up_blocks) + up_bias[None, :]
    back = blocked_sum(grad_blocks, down_blocks)
    hidden = (keep * pre).astype(jnp.bfloat16)
    grad_pre = (keep * back).astype(jnp.bfloat16)
    scale = 1.0 / math.sqrt(TOKENS)
    grad_up = (jnp.dot(tokens.T, grad_pre, preferred_element_type=jnp.float32) * scale).astype(jnp.bfloat16)
    grad_down = (jnp.dot(hidden.T, grad_out, preferred_element_type=jnp.float32) * scale).astype(jnp.bfloat16)
    grad_bias = lax.optimization_barrier(jnp.sum(grad_pre.astype(jnp.float32), axis=0)) * scale
    grad_tokens = jnp.dot(grad_pre, up_weight.T, preferred_element_type=jnp.float32).astype(jnp.bfloat16)
    return (grad_tokens, grad_up, grad_down, grad_bias)
```

```python
import functools
import math

import jax
import jax.numpy as jnp
from jax import lax
from jax.experimental import pallas as pl
from jax.experimental.pallas import tpu as pltpu
from jax.sharding import PartitionSpec as P

MESH = pl.DeviceIdType.MESH
TOK = 1024
DB = 768
FB = 3072
WIDE = 256
HALF = 128
NJ = FB // WIDE
NP = 2 * NJ
SLOTS = 12
KEEP = 1.0 / 0.9
SCALE = 1.0 / math.sqrt(TOK)
BF = jnp.bfloat16
F32 = jnp.float32
LAG_B, LAG_C, LAG_D, LAG_E, LAG_F, LAG_G, LAG_H, LAG_M = 1, 2, 3, 4, 5, 6, 7, 8


def dot_nt(left, right):
    return lax.dot_general(left, right, (((1,), (1,)), ((), ())), preferred_element_type=F32)


def kernel(
    tok_hbm, grd_hbm, up_hbm, down_hbm, bias_ref, relu_ref, drop_ref,
    gt_out, gu_out, gd_out, gb_out,
    tok, grd, tok_t, up, down, keep, acc, cols,
    part, r1, r2, summed, t1, t2, full,
    st_up, st_down, gtp, gtr, z1, z2, st_gt,
    ss, rs, ag_s, ag_r, gt_s, gt_r, loc, out_sem,
):
    row = lax.axis_index("row")
    col = lax.axis_index("col")
    x, y, z, c = row // 4, row % 4, col // 2, col % 2

    def plus(v):
        return lax.rem(v + 1, 4)

    def minus(v):
        return lax.rem(v + 3, 4)

    def far(v):
        return lax.rem(v + 2, 4)

    xp, xm = (plus(x) * 4 + y, col), (minus(x) * 4 + y, col)
    yp, ym = (x * 4 + plus(y), col), (x * 4 + minus(y), col)
    zp, zm = (row, plus(z) * 2 + c), (row, minus(z) * 2 + c)
    sib = (row, z * 2 + (1 - c))
    everyone = (xp, xm, yp, ym, zp, zm, sib)

    def remote(src, dst, s, r, dev):
        return pltpu.make_async_remote_copy(
            src_ref=src, dst_ref=dst, send_sem=s, recv_sem=r, device_id=dev, device_id_type=MESH
        )

    loads = [
        pltpu.make_async_copy(grd_hbm, grd.at[pl.ds(pl.multiple_of(col * 128, 128), 128)], loc.at[0]),
        pltpu.make_async_copy(down_hbm.at[pl.ds(0, WIDE)], down.at[pl.ds(0, WIDE)], loc.at[1]),
        pltpu.make_async_copy(down_hbm.at[pl.ds(WIDE, FB - WIDE)], down.at[pl.ds(WIDE, FB - WIDE)], loc.at[2]),
        pltpu.make_async_copy(tok_hbm, tok.at[pl.ds(pl.multiple_of(col * 128, 128), 128)], loc.at[3]),
        pltpu.make_async_copy(up_hbm, up, loc.at[4]),
    ]
    for cp in loads:
        cp.start()

    barrier = pltpu.get_barrier_semaphore()
    for dev in everyone:
        pl.semaphore_signal(barrier, inc=1, device_id=dev, device_id_type=MESH)
    pl.semaphore_wait(barrier, len(everyone))

    def block_at(buf, zz, cc, lo=0, n=128):
        return buf.at[pl.ds(pl.multiple_of((zz * 2 + cc) * 128 + lo, 64), n)]

    def gather_copies(a, src, buf):
        s, r = ag_s.at[a], ag_r.at[a]
        mine = block_at(buf, z, c)
        below, above, opp = minus(z), plus(z), far(z)
        sends = [
            (src, mine, zp),
            (src, mine, zm),
            (src, mine, sib),
            (block_at(buf, below, c, 0, 64), block_at(buf, below, c, 0, 64), zp),
            (block_at(buf, above, c, 64, 64), block_at(buf, above, c, 64, 64), zm),
            (block_at(buf, below, c), block_at(buf, below, c), sib),
            (block_at(buf, above, c), block_at(buf, above, c), sib),
            (block_at(buf, opp, c), block_at(buf, opp, c), sib),
        ]
        o = 1 - c
        lands = [
            block_at(buf, below, c), block_at(buf, above, c), block_at(buf, z, o),
            block_at(buf, opp, c, 0, 64), block_at(buf, opp, c, 64, 64),
            block_at(buf, below, o), block_at(buf, above, o), block_at(buf, opp, o),
        ]

        def send(k):
            a, b, dev = sends[k]
            return remote(a, b, s.at[k], r.at[k], dev)

        def recv(k):
            return remote(lands[k], lands[k], s.at[k], r.at[k], zp)

        return send, recv

    def gather_0(a, src, buf):
        send, _ = gather_copies(a, src, buf)
        for k in (0, 1, 2):
            send(k).start()

    def gather_1(a, src, buf):
        send, recv = gather_copies(a, src, buf)
        recv(0).wait_recv()
        send(3).start()
        recv(1).wait_recv()
        send(4).start()
        send(5).start()
        send(6).start()

    def gather_2(a, src, buf):
        send, recv = gather_copies(a, src, buf)
        recv(3).wait_recv()
        recv(4).wait_recv()
        send(7).start()

    def gather_3(a, src, buf):
        send, recv = gather_copies(a, src, buf)
        for k in (2, 5, 6, 7):
            recv(k).wait_recv()
        for k in range(8):
            send(k).wait_send()

    gather_0(0, grd_hbm, grd)

    words = relu_ref[...] & drop_ref[...]
    low = (words & 255).astype(F32).astype(BF)
    high = (words >> 8).astype(F32).astype(BF)

    def unpack(j, carry):
        word = lax.broadcasted_iota(jnp.int32, (FB // 16, WIDE), 0)
        unit = lax.broadcasted_iota(jnp.int32, (FB // 16, WIDE), 1)
        spread = (word == j * (WIDE // 16) + unit // 16).astype(F32).astype(BF)
        lows = jnp.dot(low, spread, preferred_element_type=F32).astype(jnp.int32)
        highs = jnp.dot(high, spread, preferred_element_type=F32).astype(jnp.int32)
        bit = lax.broadcasted_iota(jnp.int32, (64, WIDE), 1) % 16
        picked = jnp.where(bit < 8, lows, highs)
        on = (picked >> (bit % 8)) & 1
        keep[:, pl.ds(pl.multiple_of(j * WIDE, WIDE), WIDE)] = on.astype(F32) * KEEP
        return carry

    lax.fori_loop(0, NJ, unpack, 0)
    acc[...] = jnp.zeros_like(acc)

    gather_1(0, grd_hbm, grd)
    gather_2(0, grd_hbm, grd)
    gather_3(0, grd_hbm, grd)
    loads[0].wait()
    loads[1].wait()

    flavours = ((x, y, xp, xm, yp, ym), (y, x, yp, ym, xp, xm))

    def piece(p, f):
        d1, d2, p1, m1, p2, m2 = flavours[f]
        w = lax.rem(p, SLOTS)
        s, r = ss.at[w, f], rs.at[w, f]
        pt, sm, g = part.at[w, f], summed.at[w, f], full.at[w, f]
        ra, rb, ta, tb = r1.at[w, f], r2.at[w, f], t1.at[w, f], t2.at[w, f]
        lo, hi = pl.ds(0, 2), pl.ds(2, 2)
        lo3, hi3 = pl.ds(0, 32), pl.ds(32, 32)
        n1, b1, o1 = plus(d1), minus(d1), far(d1)
        n2, b2, o2 = plus(d2), minus(d2), far(d2)
        sends = (
            (pt.at[o1, lo], ra.at[0], p1),
            (pt.at[o1, hi], ra.at[1], m1),
            (pt.at[n1, hi], rb.at[0, hi], p1),
            (pt.at[b1, lo], rb.at[1, lo], m1),
            (pt.at[n1, lo], rb.at[0, lo], p1),
            (pt.at[b1, hi], rb.at[1, hi], m1),
            (sm.at[o2, lo3], ta.at[0], p2),
            (sm.at[o2, hi3], ta.at[1], m2),
            (sm.at[n2, hi3], tb.at[0, hi3], p2),
            (sm.at[b2, lo3], tb.at[1, lo3], m2),
            (sm.at[n2, lo3], tb.at[0, lo3], p2),
            (sm.at[b2, hi3], tb.at[1, hi3], m2),
            (g.at[d1, d2], g.at[d1, d2], p2),
            (g.at[d1, d2], g.at[d1, d2], m2),
            (g.at[d1, b2, lo3], g.at[d1, b2, lo3], p2),
            (g.at[d1, n2, hi3], g.at[d1, n2, hi3], m2),
            (g.at[d1], g.at[d1], p1),
            (g.at[d1], g.at[d1], m1),
            (g.at[b1, lo], g.at[b1, lo], p1),
            (g.at[n1, hi], g.at[n1, hi], m1),
        )
        lands = (
            ra.at[0], ra.at[1], rb.at[0, hi], rb.at[1, lo], rb.at[0, lo], rb.at[1, hi],
            ta.at[0], ta.at[1], tb.at[0, hi3], tb.at[1, lo3], tb.at[0, lo3], tb.at[1, hi3],
            g.at[d1, b2], g.at[d1, n2], g.at[d1, o2, lo3], g.at[d1, o2, hi3],
            g.at[b1], g.at[n1], g.at[o1, lo], g.at[o1, hi],
        )

        def start(*ks):
            for k in ks:
                a, b, dev = sends[k]
                remote(a, b, s.at[k], r.at[k], dev).start()

        def landed(*ks):
            for k in ks:
                remote(lands[k], lands[k], s.at[k], r.at[k], p1).wait_recv()

        def sent(*ks):
            for k in ks:
                a, b, dev = sends[k]
                remote(a, b, s.at[k], r.at[k], dev).wait_send()

        return start, landed, sent

    def when_piece(i, lag):
        p = i - lag
        return p, (p >= 0) & (p < NP)

    def forward(p, left, weight):
        w = lax.rem(p, SLOTS)
        for q in range(4):
            res = weight(left[pl.ds(q * 256, 256), :]).astype(BF)
            part[w, 0, q] = res[:, :HALF].reshape(4, 64, HALF)
            for k in range(4):
                part[w, 1, k, q] = res[k * 64 : (k + 1) * 64, HALF:]

    def stage_a(p):
        w = lax.rem(p, SLOTS)

        @pl.when(p < NJ)
        def _():
            rows = down[pl.ds(pl.multiple_of(p * WIDE, WIDE), WIDE), :]
            forward(p, grd, lambda left: dot_nt(left, rows))

        @pl.when(p >= NJ)
        def _():
            lanes = up[:, pl.ds(pl.multiple_of((p - NJ) * WIDE, WIDE), WIDE)]
            forward(p, tok, lambda left: jnp.dot(left, lanes, preferred_element_type=F32))

        for f in range(2):
            start, _, _ = piece(p, f)
            start(0, 1, 2, 3)

    def stage_b(p):
        w = lax.rem(p, SLOTS)
        for f in range(2):
            d1 = flavours[f][0]
            start, landed, _ = piece(p, f)
            landed(0, 1)
            n1, b1 = plus(d1), minus(d1)
            part[w, f, n1, 0:2] = (part[w, f, n1, 0:2].astype(F32) + r1[w, f, 0].astype(F32)).astype(BF)
            part[w, f, b1, 2:4] = (part[w, f, b1, 2:4].astype(F32) + r1[w, f, 1].astype(F32)).astype(BF)
            start(4, 5)

    def stage_c(p):
        w = lax.rem(p, SLOTS)
        for f in range(2):
            d1 = flavours[f][0]
            start, landed, _ = piece(p, f)
            landed(2, 3, 4, 5)
            total = part[w, f, d1].astype(F32) + r2[w, f, 0].astype(F32) + r2[w, f, 1].astype(F32)
            summed[w, f] = total.astype(BF)
            start(6, 7, 8, 9)

    def stage_d(p):
        w = lax.rem(p, SLOTS)
        for f in range(2):
            d2 = flavours[f][1]
            start, landed, _ = piece(p, f)
            landed(6, 7)
            n2, b2 = plus(d2), minus(d2)
            summed[w, f, n2, 0:32] = (summed[w, f, n2, 0:32].astype(F32) + t1[w, f, 0].astype(F32)).astype(BF)
            summed[w, f, b2, 32:64] = (summed[w, f, b2, 32:64].astype(F32) + t1[w, f, 1].astype(F32)).astype(BF)
            start(10, 11)

    def stage_e(p):
        w = lax.rem(p, SLOTS)
        j = lax.rem(p, NJ)
        on_pre = (p >= NJ).astype(F32)
        for f in range(2):
            d1, d2 = flavours[f][:2]
            start, landed, sent = piece(p, f)
            landed(8, 9, 10, 11)
            total = summed[w, f, d2].astype(F32) + t2[w, f, 0].astype(F32) + t2[w, f, 1].astype(F32)
            lanes = pl.ds(pl.multiple_of(j * WIDE + f * HALF, HALF), HALF)
            total = total + bias_ref[0:1, lanes] * on_pre
            full[w, f, d1, d2] = (keep[:, lanes] * total).astype(BF)
            start(12, 13)
            sent(0, 1, 2, 3, 4, 5)

    def stage_f(p):
        for f in range(2):
            start, landed, _ = piece(p, f)
            landed(12, 13)
            start(14, 15)

    def stage_g(p):
        for f in range(2):
            start, landed, sent = piece(p, f)
            landed(14, 15)
            start(16, 17)
            sent(6, 7, 8, 9, 10, 11)

    def stage_h(p):
        for f in range(2):
            start, landed, _ = piece(p, f)
            landed(16, 17)
            start(18, 19)

    def store_up(j):
        w = lax.rem(j, 2)
        lanes = pl.ds(pl.multiple_of(j * WIDE, WIDE), WIDE)
        return pltpu.make_async_copy(st_up.at[w], gu_out.at[:, lanes], out_sem.at[w])

    def store_down(j):
        w = lax.rem(j, 2)
        rows = pl.ds(pl.multiple_of(j * WIDE, WIDE), WIDE)
        return pltpu.make_async_copy(st_down.at[w], gd_out.at[rows], out_sem.at[2 + w])

    def stage_m(p):
        w = lax.rem(p, SLOTS)
        for f in range(2):
            _, landed, _ = piece(p, f)
            landed(18, 19)
        cols[:, :HALF] = full[w, 0].reshape(TOK, HALF)
        for q in range(4):
            for k in range(4):
                cols[(q * 4 + k) * 64 : (q * 4 + k + 1) * 64, HALF:] = full[w, 1, k, q]

        @pl.when(p < NJ)
        def _():
            j = p
            lanes = pl.ds(pl.multiple_of(j * WIDE, WIDE), WIDE)

            @pl.when(j >= 2)
            def _():
                store_up(j).wait()

            for q in range(3):
                res = jnp.dot(tok_t[q * 256 : (q + 1) * 256, :], cols[...], preferred_element_type=F32)
                st_up[lax.rem(j, 2), q * 256 : (q + 1) * 256, :] = (res * SCALE).astype(BF)
            store_up(j).start()
            gb_out[0:1, lanes] = jnp.sum(cols[...].astype(F32), axis=0, keepdims=True) * SCALE
            for q in range(4):
                acc[q * 256 : (q + 1) * 256, :] += dot_nt(cols[q * 256 : (q + 1) * 256, :], up[:, lanes])

        @pl.when(p >= NJ)
        def _():
            j = p - NJ

            @pl.when(j >= 2)
            def _():
                store_down(j).wait()

            res = lax.dot_general(cols[...], grd[...], (((0,), (0,)), ((), ())), preferred_element_type=F32)
            st_down[lax.rem(j, 2)] = (res * SCALE).astype(BF)
            store_down(j).start()

        for f in range(2):
            _, _, sent = piece(p, f)
            sent(12, 13, 14, 15, 16, 17, 18, 19)

    def gt_copies():
        s, r = gt_s, gt_r
        mine = gtp.at[c]
        above, below, opp = plus(z), minus(z), far(z)
        lo, hi = pl.ds(0, 64), pl.ds(64, 64)
        sends = [
            (gtp.at[1 - c], gtr, sib),
            (mine.at[opp, lo], z1.at[0], zp),
            (mine.at[opp, hi], z1.at[1], zm),
            (mine.at[above, hi], z2.at[0, hi], zp),
            (mine.at[below, lo], z2.at[1, lo], zm),
            (mine.at[above, lo], z2.at[0, lo], zp),
            (mine.at[below, hi], z2.at[1, hi], zm),
        ]

        def send(k):
            a, b, dev = sends[k]
            return remote(a, b, s.at[k], r.at[k], dev)

        return send

    def gt_0():
        for q in range(8):
            gtp[q % 2, q // 2] = acc[q * 128 : (q + 1) * 128, :].astype(BF)
        gt_copies()(0).start()

    def gt_1():
        send = gt_copies()
        send(0).wait_recv()
        for q in range(4):
            gtp[c, q] = (gtp[c, q].astype(F32) + gtr[q].astype(F32)).astype(BF)
        for k in (1, 2, 3, 4):
            send(k).start()

    def gt_2():
        send = gt_copies()
        send(1).wait_recv()
        send(2).wait_recv()
        above, below = plus(z), minus(z)
        gtp[c, above, 0:64] = (gtp[c, above, 0:64].astype(F32) + z1[0].astype(F32)).astype(BF)
        gtp[c, below, 64:128] = (gtp[c, below, 64:128].astype(F32) + z1[1].astype(F32)).astype(BF)
        send(5).start()
        send(6).start()

    def gt_3():
        send = gt_copies()
        for k in (3, 4, 5, 6):
            send(k).wait_recv()
        st_gt[...] = (gtp[c, z].astype(F32) + z2[0].astype(F32) + z2[1].astype(F32)).astype(BF)
        cp = pltpu.make_async_copy(st_gt, gt_out, out_sem.at[4])
        cp.start()
        for k in range(7):
            send(k).wait_send()
        cp.wait()

    def step(i, carry):
        for fn, lag in (
            (stage_h, LAG_H), (stage_g, LAG_G), (stage_f, LAG_F), (stage_e, LAG_E),
            (stage_d, LAG_D), (stage_c, LAG_C), (stage_b, LAG_B), (stage_a, 0), (stage_m, LAG_M),
        ):
            p, on = when_piece(i, lag)
            pl.when(on)(functools.partial(fn, p))

        def at(n):
            return pl.when(i == n)

        @at(0)
        def _():
            loads[2].wait()
            gather_0(1, tok_hbm, tok)

        @at(2)
        def _():
            gather_1(1, tok_hbm, tok)

        @at(4)
        def _():
            gather_2(1, tok_hbm, tok)

        @at(6)
        def _():
            gather_3(1, tok_hbm, tok)
            loads[3].wait()
            loads[4].wait()
            for q in range(8):
                tok_t[:, q * 128 : (q + 1) * 128] = tok[q * 128 : (q + 1) * 128, :].T

        last = LAG_M + NJ - 1
        at(last)(gt_0)
        at(last + 2)(gt_1)
        at(last + 4)(gt_2)
        at(last + 7)(gt_3)
        return carry

    lax.fori_loop(0, NP + LAG_M, step, 0)
    for j in (NJ - 2, NJ - 1):
        store_up(j).wait()
        store_down(j).wait()


def body(tokens, grad_out, up_weight, down_weight, up_bias, relu_bits, drop_bits):
    hbm = pl.BlockSpec(memory_space=pl.ANY)
    vmem = pl.BlockSpec(memory_space=pltpu.VMEM)
    dma = pltpu.SemaphoreType.DMA
    gt, gu, gd, gb = pl.pallas_call(
        kernel,
        out_shape=(
            jax.ShapeDtypeStruct((128, DB), BF),
            jax.ShapeDtypeStruct((DB, FB), BF),
            jax.ShapeDtypeStruct((FB, DB), BF),
            jax.ShapeDtypeStruct((1, FB), F32),
        ),
        in_specs=[hbm, hbm, hbm, hbm, vmem, vmem, vmem],
        out_specs=(hbm, hbm, hbm, vmem),
        scratch_shapes=[
            pltpu.VMEM((TOK, DB), BF),
            pltpu.VMEM((TOK, DB), BF),
            pltpu.VMEM((DB, TOK), BF),
            pltpu.VMEM((DB, FB), BF),
            pltpu.VMEM((FB, DB), BF),
            pltpu.VMEM((64, FB), F32),
            pltpu.VMEM((TOK, DB), F32),
            pltpu.VMEM((TOK, WIDE), BF),
            pltpu.VMEM((SLOTS, 2, 4, 4, 64, HALF), BF),
            pltpu.VMEM((SLOTS, 2, 2, 2, 64, HALF), BF),
            pltpu.VMEM((SLOTS, 2, 2, 4, 64, HALF), BF),
            pltpu.VMEM((SLOTS, 2, 4, 64, HALF), BF),
            pltpu.VMEM((SLOTS, 2, 2, 32, HALF), BF),
            pltpu.VMEM((SLOTS, 2, 2, 64, HALF), BF),
            pltpu.VMEM((SLOTS, 2, 4, 4, 64, HALF), BF),
            pltpu.VMEM((2, DB, WIDE), BF),
            pltpu.VMEM((2, WIDE, DB), BF),
            pltpu.VMEM((2, 4, 128, DB), BF),
            pltpu.VMEM((4, 128, DB), BF),
            pltpu.VMEM((2, 64, DB), BF),
            pltpu.VMEM((2, 128, DB), BF),
            pltpu.VMEM((128, DB), BF),
            dma((SLOTS, 2, 20)),
            dma((SLOTS, 2, 20)),
            dma((2, 8)),
            dma((2, 8)),
            dma((7,)),
            dma((7,)),
            dma((5,)),
            dma((5,)),
        ],
        compiler_params=pltpu.CompilerParams(
            collective_id=0, has_side_effects=True, vmem_limit_bytes=60 * 2**20
        ),
        cost_estimate=pl.CostEstimate(
            flops=10 * TOK * DB * FB, bytes_accessed=10 * DB * FB, transcendentals=0
        ),
        name="fused",
    )(tokens, grad_out, up_weight, down_weight, up_bias.reshape(1, FB), relu_bits, drop_bits)
    return gt, gu, gd, gb.reshape(FB)


def solution(mesh):
    return jax.shard_map(
        body,
        mesh=mesh,
        in_specs=(
            P("col", "row"), P("col", "row"), P("row", "col"), P("col", "row"),
            P("col"), P("row", "col"), P("row", "col"),
        ),
        out_specs=(P("col", "row"), P("row", "col"), P("col", "row"), P("col")),
        check_vma=False,
    )
```

```python
import functools
import math

import jax
import jax.numpy as jnp
from jax import lax
from jax.experimental import pallas as pl
from jax.experimental.pallas import tpu as pltpu
from jax.sharding import PartitionSpec as P

MESH = pl.DeviceIdType.MESH
TOK = 1024
DB = 768
FB = 3072
WIDE = 256
HALF = 128
NJ = FB // WIDE
NP = 2 * NJ
RING = 16
HELD = 16
EARLY = 8
SLACK = 1
KEEP = 1.0 / 0.9
SCALE = 1.0 / math.sqrt(TOK)
BF = jnp.bfloat16
F32 = jnp.float32
GROUP = (0, 0, 1, 1, 1, 1, 2, 2, 3, 3, 3, 3, 4, 4, 5, 5, 6, 6, 7, 7)
LAG_A, LAG_B, LAG_C, LAG_D, LAG_E, LAG_F, LAG_G, LAG_H, LAG_M = -EARLY, 0, 2, 4, 6, 8, 10, 12, 14


def dot_nt(left, right):
    return lax.dot_general(left, right, (((1,), (1,)), ((), ())), preferred_element_type=F32)


def kernel(
    tok_hbm, grd_hbm, up_hbm, down_hbm, bias_hbm, relu_hbm, drop_hbm,
    gt_out, gu_out, gd_out, gb_out,
    tok, grd, tok_t, up, down, keep, acc, cols,
    part, r1, r2, summed, t1, t2, full,
    gtp, gtr, z1, z2, words, dropped, swapped, bias,
    ss, rs, ag_s, ag_r, gt_s, gt_r, sw_s, sw_r, pace, loc,
):
    row = lax.axis_index("row")
    col = lax.axis_index("col")
    x, y, z, c = row // 4, row % 4, col // 2, col % 2

    def plus(v):
        return lax.rem(v + 1, 4)

    def minus(v):
        return lax.rem(v + 3, 4)

    def far(v):
        return lax.rem(v + 2, 4)

    xp, xm = (plus(x) * 4 + y, col), (minus(x) * 4 + y, col)
    yp, ym = (x * 4 + plus(y), col), (x * 4 + minus(y), col)
    zp, zm = (row, plus(z) * 2 + c), (row, minus(z) * 2 + c)
    sib = (row, z * 2 + (1 - c))
    everyone = (xp, xm, yp, ym, zp, zm, sib)

    def remote(src, dst, s, r, dev):
        return pltpu.make_async_remote_copy(
            src_ref=src, dst_ref=dst, send_sem=s, recv_sem=r, device_id=dev, device_id_type=MESH
        )

    third = FB // 3
    loads = [
        pltpu.make_async_copy(grd_hbm, grd.at[pl.ds(pl.multiple_of(col * 128, 128), 128)], loc.at[0]),
        pltpu.make_async_copy(down_hbm.at[pl.ds(0, third)], down.at[pl.ds(0, third)], loc.at[1]),
        pltpu.make_async_copy(down_hbm.at[pl.ds(third, 2 * third)], down.at[pl.ds(third, 2 * third)], loc.at[2]),
        pltpu.make_async_copy(tok_hbm, tok.at[pl.ds(pl.multiple_of(col * 128, 128), 128)], loc.at[3]),
        pltpu.make_async_copy(up_hbm, up, loc.at[4]),
        pltpu.make_async_copy(relu_hbm, words, loc.at[5]),
        pltpu.make_async_copy(drop_hbm, dropped, loc.at[6]),
        pltpu.make_async_copy(bias_hbm, bias, loc.at[7]),
    ]
    for k in (0, 1, 5, 6):
        loads[k].start()

    barrier = pltpu.get_barrier_semaphore()
    for dev in everyone:
        pl.semaphore_signal(barrier, inc=1, device_id=dev, device_id_type=MESH)
    mirror = (y * 4 + x, col)

    @pl.when(x != y)
    def _():
        pl.semaphore_signal(barrier, inc=1, device_id=mirror, device_id_type=MESH)

    pl.semaphore_wait(barrier, len(everyone) + (x != y).astype(jnp.int32))

    def block_at(buf, zz, cc, lo=0, n=128):
        return buf.at[pl.ds(pl.multiple_of((zz * 2 + cc) * 128 + lo, 64), n)]

    def gather_copies(a, src, buf):
        s, r = ag_s.at[a], ag_r.at[a]
        mine = block_at(buf, z, c)
        below, above, opp = minus(z), plus(z), far(z)
        lower, upper = block_at(buf, z, c, 0, 64), block_at(buf, z, c, 64, 64)
        src_lower, src_upper = src.at[pl.ds(0, 64)], src.at[pl.ds(64, 64)]
        far_lower, far_upper = block_at(buf, opp, c, 0, 64), block_at(buf, opp, c, 64, 64)
        sends = [
            (src_lower, lower, zp),
            (src_upper, upper, zp),
            (src_upper, upper, zm),
            (src_lower, lower, zm),
            (src, mine, sib),
            (block_at(buf, below, c, 0, 64), block_at(buf, below, c, 0, 64), zp),
            (block_at(buf, above, c, 64, 64), block_at(buf, above, c, 64, 64), zm),
            (block_at(buf, below, c), block_at(buf, below, c), sib),
            (block_at(buf, above, c), block_at(buf, above, c), sib),
            (far_lower, far_lower, sib),
            (far_upper, far_upper, sib),
        ]
        o = 1 - c
        lands = [
            block_at(buf, below, c, 0, 64), block_at(buf, below, c, 64, 64),
            block_at(buf, above, c, 64, 64), block_at(buf, above, c, 0, 64),
            block_at(buf, z, o),
            far_lower, far_upper,
            block_at(buf, below, o), block_at(buf, above, o),
            block_at(buf, opp, o, 0, 64), block_at(buf, opp, o, 64, 64),
        ]

        def send(k):
            a, b, dev = sends[k]
            return remote(a, b, s.at[k], r.at[k], dev)

        def recv(k):
            return remote(lands[k], lands[k], s.at[k], r.at[k], zp)

        return send, recv

    def gather_0(a, src, buf):
        send, _ = gather_copies(a, src, buf)
        for k in (4, 0, 2, 1, 3):
            send(k).start()

    def gather_1(a, src, buf):
        send, recv = gather_copies(a, src, buf)
        for got, on in ((0, 5), (2, 6), (1, 7), (3, 8)):
            recv(got).wait_recv()
            send(on).start()

    def gather_2(a, src, buf):
        send, recv = gather_copies(a, src, buf)
        for got, on in ((5, 9), (6, 10)):
            recv(got).wait_recv()
            send(on).start()

    def gather_3(a, src, buf):
        send, recv = gather_copies(a, src, buf)
        for k in (4, 7, 8, 9, 10):
            recv(k).wait_recv()
        for k in range(11):
            send(k).wait_send()

    gather_0(0, grd_hbm, grd)
    for k in (2, 7):
        loads[k].start()

    swap = remote(words, swapped, sw_s, sw_r, mirror)
    loads[5].wait()
    loads[6].wait()
    words[...] = words[...] & dropped[...]

    @pl.when(x != y)
    def _():
        swap.start()

    @pl.when(x == y)
    def _():
        swapped[...] = words[...]

    def unpack(j):
        word = lax.broadcasted_iota(jnp.int32, (FB // 16, HALF), 0)
        unit = lax.broadcasted_iota(jnp.int32, (FB // 16, HALF), 1)
        bit = lax.broadcasted_iota(jnp.int32, (64, HALF), 1) % 16
        for f, ref in enumerate((swapped, words)):
            got = ref[...]
            low = (got & 255).astype(F32).astype(BF)
            high = (got >> 8).astype(F32).astype(BF)
            spread = (word == (j * WIDE + f * HALF + unit) // 16).astype(F32).astype(BF)
            lows = jnp.dot(low, spread, preferred_element_type=F32).astype(jnp.int32)
            highs = jnp.dot(high, spread, preferred_element_type=F32).astype(jnp.int32)
            picked = jnp.where(bit < 8, lows, highs)
            on = (picked >> (bit % 8)) & 1
            keep[:, pl.ds(pl.multiple_of(j * WIDE + f * HALF, HALF), HALF)] = on.astype(F32) * KEEP

    flavours = ((x, y, xp, xm, yp, ym), (y, x, yp, ym, xp, xm))

    def forward_block(p, left, weight, q):
        w = lax.rem(p, RING)
        res = weight(left[pl.ds(pl.multiple_of(q * 256, 256), 256), :]).astype(BF)
        for f in range(2):
            for k in range(4):
                part[w, f, k, q] = res[k * 64 : (k + 1) * 64, f * HALF : (f + 1) * HALF]

    def early(q, first=0, end=EARLY):
        top = q // 2

        def one(p, carry):
            rows = down[pl.ds(pl.multiple_of(p * WIDE, WIDE), WIDE), :]
            forward_block(p, grd, lambda left: dot_nt(left, rows), q)
            for f in range(2):
                d1 = flavours[f][0]
                pt, ra, rb, s, r = part.at[p, f], r1.at[p, f], r2.at[p, f], ss.at[p, f], rs.at[p, f]

                def along(off):
                    to = lax.rem(d1 + off, 4)
                    return to, ((to * 4 + y, col) if f == 0 else (x * 4 + to, col))

                _, dev = along(1 + 2 * top)
                remote(pt.at[far(d1), q], ra.at[top, q - 2 * top], s.at[0], r.at[0], dev).start()
                to, dev = along(3 - 2 * top)
                remote(pt.at[to, q], rb.at[1 - top, q], s.at[0], r.at[1], dev).start()
            return carry

        lax.fori_loop(first, end, one, 0)

    loads[0].wait()
    loads[1].wait()
    send, recv = gather_copies(0, grd_hbm, grd)
    recv(4).wait_recv()
    early(z, 0, EARLY // 2)
    for got, on in ((0, 5), (2, 6)):
        recv(got).wait_recv()
        send(on).start()
    loads[2].wait()
    early(z, EARLY // 2, EARLY)
    for got, on in ((1, 7), (3, 8)):
        recv(got).wait_recv()
        send(on).start()
    gather_0(1, tok_hbm, tok)
    loads[3].start()
    loads[4].start()
    recv(7).wait_recv()
    early(minus(z))
    for got, on in ((5, 9), (6, 10)):
        recv(got).wait_recv()
        send(on).start()
    recv(8).wait_recv()
    early(plus(z))
    for k in (9, 10):
        recv(k).wait_recv()
    early(far(z))
    for k in range(11):
        send(k).wait_send()
    loads[7].wait()

    def piece(p, f):
        d1, d2, p1, m1, p2, m2 = flavours[f]
        w, v = lax.rem(p, RING), lax.rem(p, HELD)
        s, r = ss.at[v, f], rs.at[v, f]
        pt, sm, g = part.at[w, f], summed.at[w, f], full.at[v, f]
        ra, rb, ta, tb = r1.at[w, f], r2.at[w, f], t1.at[w, f], t2.at[w, f]
        lo, hi = pl.ds(0, 2), pl.ds(2, 2)
        lo3, hi3 = pl.ds(0, 32), pl.ds(32, 32)
        n1, b1, o1 = plus(d1), minus(d1), far(d1)
        n2, b2, o2 = plus(d2), minus(d2), far(d2)
        sends = (
            (pt.at[o1, lo], ra.at[0], p1),
            (pt.at[o1, hi], ra.at[1], m1),
            (pt.at[n1, hi], rb.at[0, hi], p1),
            (pt.at[b1, lo], rb.at[1, lo], m1),
            (pt.at[n1, lo], rb.at[0, lo], p1),
            (pt.at[b1, hi], rb.at[1, hi], m1),
            (sm.at[o2, lo3], ta.at[0], p2),
            (sm.at[o2, hi3], ta.at[1], m2),
            (sm.at[n2, hi3], tb.at[0, hi3], p2),
            (sm.at[b2, lo3], tb.at[1, lo3], m2),
            (sm.at[n2, lo3], tb.at[0, lo3], p2),
            (sm.at[b2, hi3], tb.at[1, hi3], m2),
            (g.at[d1, d2], g.at[d1, d2], p2),
            (g.at[d1, d2], g.at[d1, d2], m2),
            (g.at[d1, b2, lo3], g.at[d1, b2, lo3], p2),
            (g.at[d1, n2, hi3], g.at[d1, n2, hi3], m2),
            (g.at[d1], g.at[d1], p1),
            (g.at[d1], g.at[d1], m1),
            (g.at[b1, lo], g.at[b1, lo], p1),
            (g.at[n1, hi], g.at[n1, hi], m1),
        )
        lands = (ra, rb, ta, tb, g.at[o1, lo], g.at[d1, o2], g.at[pl.ds(0, 2)], g.at[o1])

        def start(*ks):
            for k in ks:
                a, b, dev = sends[k]
                remote(a, b, s.at[min(k // 6, 2)], r.at[GROUP[k]], dev).start()

        def landed(n):
            remote(lands[n], lands[n], s.at[0], r.at[n], p1).wait_recv()

        def sent(n):
            some = grd.at[pl.ds(0, (128, 32, 160)[n])]
            remote(some, some, s.at[n], r.at[0], p1).wait_send()

        return start, landed, sent

    def when_piece(i, lag):
        p = i - lag
        return p, (p >= 0) & (p < NP)

    def forward(p, left, weight):
        for q in range(4):
            forward_block(p, left, weight, q)

    def stage_a(p):

        @pl.when(p < NJ)
        def _():
            rows = down[pl.ds(pl.multiple_of(p * WIDE, WIDE), WIDE), :]
            forward(p, grd, lambda left: dot_nt(left, rows))

        @pl.when(p >= NJ)
        def _():
            lanes = up[:, pl.ds(pl.multiple_of((p - NJ) * WIDE, WIDE), WIDE)]
            forward(p, tok, lambda left: jnp.dot(left, lanes, preferred_element_type=F32))

        for f in range(2):
            start, _, _ = piece(p, f)
            start(0, 1, 2, 3)

    def stage_b(p):
        w = lax.rem(p, RING)
        for f in range(2):
            d1 = flavours[f][0]
            start, landed, _ = piece(p, f)
            landed(0)
            n1, b1 = plus(d1), minus(d1)
            part[w, f, n1, 0:2] = (part[w, f, n1, 0:2].astype(F32) + r1[w, f, 0].astype(F32)).astype(BF)
            part[w, f, b1, 2:4] = (part[w, f, b1, 2:4].astype(F32) + r1[w, f, 1].astype(F32)).astype(BF)
            start(4, 5)

    def stage_c(p):
        w = lax.rem(p, RING)
        for f in range(2):
            d1 = flavours[f][0]
            start, landed, _ = piece(p, f)
            landed(1)
            total = part[w, f, d1].astype(F32) + r2[w, f, 0].astype(F32) + r2[w, f, 1].astype(F32)
            summed[w, f] = total.astype(BF)
            start(6, 7, 8, 9)

    def stage_d(p):
        w = lax.rem(p, RING)
        for f in range(2):
            d2 = flavours[f][1]
            start, landed, _ = piece(p, f)
            landed(2)
            n2, b2 = plus(d2), minus(d2)
            summed[w, f, n2, 0:32] = (summed[w, f, n2, 0:32].astype(F32) + t1[w, f, 0].astype(F32)).astype(BF)
            summed[w, f, b2, 32:64] = (summed[w, f, b2, 32:64].astype(F32) + t1[w, f, 1].astype(F32)).astype(BF)
            start(10, 11)

    def stage_e(p):
        w, v = lax.rem(p, RING), lax.rem(p, HELD)
        j = lax.rem(p, NJ)
        on_pre = (p >= NJ).astype(F32)
        for f in range(2):
            d1, d2 = flavours[f][:2]
            start, landed, sent = piece(p, f)
            landed(3)
            total = summed[w, f, d2].astype(F32) + t2[w, f, 0].astype(F32) + t2[w, f, 1].astype(F32)
            lanes = pl.ds(pl.multiple_of(j * WIDE + f * HALF, HALF), HALF)
            total = total + bias[0:1, lanes] * on_pre
            full[v, f, d1, d2] = (keep[:, lanes] * total).astype(BF)
            start(12, 13)
            sent(0)

    def stage_f(p):
        for f in range(2):
            start, landed, _ = piece(p, f)
            landed(4)
            start(14, 15)

    def stage_g(p):
        for f in range(2):
            start, landed, sent = piece(p, f)
            landed(5)
            start(16, 17)
            sent(1)

    def stage_h(p):
        for f in range(2):
            start, landed, _ = piece(p, f)
            landed(6)
            start(18, 19)

    def stage_m(p):
        w = lax.rem(p, HELD)
        for f in range(2):
            _, landed, _ = piece(p, f)
            landed(7)
        for f in range(2):
            for q in range(4):
                for k in range(4):
                    cols[(q * 4 + k) * 64 : (q * 4 + k + 1) * 64, f * HALF : (f + 1) * HALF] = full[w, f, k, q]

        @pl.when(p < NJ)
        def _():
            j = p
            lanes = pl.ds(pl.multiple_of(j * WIDE, WIDE), WIDE)

            for q in range(3):
                res = jnp.dot(tok_t[q * 256 : (q + 1) * 256, :], cols[...], preferred_element_type=F32)
                gu_out[q * 256 : (q + 1) * 256, lanes] = (res * SCALE).astype(BF)
            gb_out[0:1, lanes] = jnp.sum(cols[...].astype(F32), axis=0, keepdims=True) * SCALE
            for q in range(4):
                acc[q * 256 : (q + 1) * 256, :] += dot_nt(cols[q * 256 : (q + 1) * 256, :], up[:, lanes])

        @pl.when(p >= NJ)
        def _():
            j = p - NJ

            res = lax.dot_general(cols[...], grd[...], (((0,), (0,)), ((), ())), preferred_element_type=F32)
            gd_out[pl.ds(pl.multiple_of(j * WIDE, WIDE), WIDE), :] = (res * SCALE).astype(BF)

        for f in range(2):
            _, _, sent = piece(p, f)
            sent(2)

    def gt_copies():
        s, r = gt_s, gt_r
        mine = gtp.at[c]
        above, below, opp = plus(z), minus(z), far(z)
        lo, hi = pl.ds(0, 64), pl.ds(64, 64)
        sends = [
            (gtp.at[1 - c], gtr, sib),
            (mine.at[opp, lo], z1.at[0], zp),
            (mine.at[opp, hi], z1.at[1], zm),
            (mine.at[above, hi], z2.at[0, hi], zp),
            (mine.at[below, lo], z2.at[1, lo], zm),
            (mine.at[above, lo], z2.at[0, lo], zp),
            (mine.at[below, hi], z2.at[1, hi], zm),
        ]

        def send(k):
            a, b, dev = sends[k]
            return remote(a, b, s.at[k], r.at[k], dev)

        return send

    def gt_0():
        for q in range(8):
            gtp[q % 2, q // 2] = acc[q * 128 : (q + 1) * 128, :].astype(BF)
        gt_copies()(0).start()

    def gt_1():
        send = gt_copies()
        send(0).wait_recv()
        for q in range(4):
            gtp[c, q] = (gtp[c, q].astype(F32) + gtr[q].astype(F32)).astype(BF)
        for k in (1, 2, 3, 4):
            send(k).start()

    def gt_2():
        send = gt_copies()
        send(1).wait_recv()
        send(2).wait_recv()
        above, below = plus(z), minus(z)
        gtp[c, above, 0:64] = (gtp[c, above, 0:64].astype(F32) + z1[0].astype(F32)).astype(BF)
        gtp[c, below, 64:128] = (gtp[c, below, 64:128].astype(F32) + z1[1].astype(F32)).astype(BF)
        send(5).start()
        send(6).start()

    def gt_3():
        send = gt_copies()
        for k in (3, 4, 5, 6):
            send(k).wait_recv()
        gt_out[...] = (gtp[c, z].astype(F32) + z2[0].astype(F32) + z2[1].astype(F32)).astype(BF)
        for k in range(7):
            send(k).wait_send()

    def step(i, carry):
        @pl.when(i >= SLACK)
        def _():
            pl.semaphore_wait(pace, 1)

        for fn, lag in (
            (stage_h, LAG_H), (stage_g, LAG_G), (stage_f, LAG_F), (stage_e, LAG_E),
            (stage_d, LAG_D), (stage_c, LAG_C), (stage_b, LAG_B), (stage_a, LAG_A), (stage_m, LAG_M),
        ):
            p, on = when_piece(i, lag)
            on = on & (p >= EARLY) if fn is stage_a else on
            pl.when(on)(functools.partial(fn, p))

        def at(n):
            return pl.when(i == n)

        @pl.when((i == 0) & (x != y))
        def _():
            swap.wait()

        pl.when(i < NJ)(functools.partial(unpack, i))

        @at(0)
        def _():
            gather_1(1, tok_hbm, tok)
            acc[...] = jnp.zeros_like(acc)

        @at(2)
        def _():
            gather_2(1, tok_hbm, tok)
            loads[3].wait()
            loads[4].wait()

        @at(3)
        def _():
            gather_3(1, tok_hbm, tok)

        @at(6)
        def _():
            for q in range(8):
                tok_t[:, q * 128 : (q + 1) * 128] = tok[q * 128 : (q + 1) * 128, :].T

        last = LAG_M + NJ - 1
        at(last)(gt_0)
        at(last + 2)(gt_1)
        at(last + 4)(gt_2)
        at(last + 7)(gt_3)
        pl.semaphore_signal(pace, inc=1, device_id=sib, device_id_type=MESH)
        return carry

    lax.fori_loop(0, NP + LAG_M, step, 0)
    pl.semaphore_wait(pace, SLACK)


def flush(gt, gu, gd, gb, gt_out, gu_out, gd_out, gb_out, sem):
    copies = [pltpu.make_async_copy(gt, gt_out, sem.at[0]), pltpu.make_async_copy(gb, gb_out, sem.at[1])]
    for q in range(4):
        rows = pl.ds(q * DB // 4, DB // 4)
        copies.append(pltpu.make_async_copy(gu.at[rows], gu_out.at[rows], sem.at[2 + q]))
        rows = pl.ds(q * FB // 4, FB // 4)
        copies.append(pltpu.make_async_copy(gd.at[rows], gd_out.at[rows], sem.at[6 + q]))
    for cp in copies:
        cp.start()
    for cp in copies:
        cp.wait()


def body(tokens, grad_out, up_weight, down_weight, up_bias, relu_bits, drop_bits):
    hbm = pl.BlockSpec(memory_space=pl.ANY)
    vmem = pl.BlockSpec(memory_space=pltpu.VMEM)
    dma = pltpu.SemaphoreType.DMA
    shapes = (((128, DB), BF), ((DB, FB), BF), ((FB, DB), BF), ((1, FB), F32))
    held = pl.pallas_call(
        kernel,
        out_shape=tuple(pltpu.VMEM(shape, dtype) for shape, dtype in shapes),
        in_specs=[hbm] * 7,
        out_specs=(vmem,) * 4,
        scratch_shapes=[
            pltpu.VMEM((TOK, DB), BF),
            pltpu.VMEM((TOK, DB), BF),
            pltpu.VMEM((DB, TOK), BF),
            pltpu.VMEM((DB, FB), BF),
            pltpu.VMEM((FB, DB), BF),
            pltpu.VMEM((64, FB), F32),
            pltpu.VMEM((TOK, DB), F32),
            pltpu.VMEM((TOK, WIDE), BF),
            pltpu.VMEM((RING, 2, 4, 4, 64, HALF), BF),
            pltpu.VMEM((RING, 2, 2, 2, 64, HALF), BF),
            pltpu.VMEM((RING, 2, 2, 4, 64, HALF), BF),
            pltpu.VMEM((RING, 2, 4, 64, HALF), BF),
            pltpu.VMEM((RING, 2, 2, 32, HALF), BF),
            pltpu.VMEM((RING, 2, 2, 64, HALF), BF),
            pltpu.VMEM((HELD, 2, 4, 4, 64, HALF), BF),
            pltpu.VMEM((2, 4, 128, DB), BF),
            pltpu.VMEM((4, 128, DB), BF),
            pltpu.VMEM((2, 64, DB), BF),
            pltpu.VMEM((2, 128, DB), BF),
            pltpu.VMEM((64, FB // 16), jnp.int32),
            pltpu.VMEM((64, FB // 16), jnp.int32),
            pltpu.VMEM((64, FB // 16), jnp.int32),
            pltpu.VMEM((1, FB), F32),
            dma((HELD, 2, 3)),
            dma((HELD, 2, 8)),
            dma((2, 11)),
            dma((2, 11)),
            dma((7,)),
            dma((7,)),
            dma,
            dma,
            pltpu.SemaphoreType.REGULAR,
            dma((8,)),
        ],
        compiler_params=pltpu.CompilerParams(
            collective_id=0, has_side_effects=True, vmem_limit_bytes=48 * 2**20
        ),
        cost_estimate=pl.CostEstimate(
            flops=10 * TOK * DB * FB, bytes_accessed=10 * DB * FB, transcendentals=0
        ),
        name="fused",
    )(tokens, grad_out, up_weight, down_weight, up_bias.reshape(1, FB), relu_bits, drop_bits)
    gt, gu, gd, gb = pl.pallas_call(
        flush,
        out_shape=tuple(jax.ShapeDtypeStruct(shape, dtype) for shape, dtype in shapes),
        in_specs=[vmem] * 4,
        out_specs=(hbm,) * 4,
        scratch_shapes=[dma((10,))],
        compiler_params=pltpu.CompilerParams(vmem_limit_bytes=2**20),
        name="flush",
    )(*held)
    return gt, gu, gd, gb.reshape(FB)


def solution(mesh):
    return jax.shard_map(
        body,
        mesh=mesh,
        in_specs=(
            P("col", "row"), P("col", "row"), P("row", "col"), P("col", "row"),
            P("col"), P("row", "col"), P("row", "col"),
        ),
        out_specs=(P("col", "row"), P("row", "col"), P("col", "row"), P("col")),
        check_vma=False,
    )
```

```python
import functools
import math

import jax
import jax.numpy as jnp
from jax import lax
from jax.experimental import pallas as pl
from jax.experimental.pallas import tpu as pltpu
from jax.sharding import PartitionSpec as P

MESH = pl.DeviceIdType.MESH
TOK = 1024
DB = 768
FB = 3072
WIDE = 256
HALF = 128
NJ = FB // WIDE
NP = 2 * NJ
RING = 16
HELD = 16
EARLY = 8
KEEP = 1.0 / 0.9
SCALE = 1.0 / math.sqrt(TOK)
BF = jnp.bfloat16
F32 = jnp.float32
GROUP = (0, 0, 1, 1, 1, 1, 2, 2, 3, 3, 3, 3, 4, 4, 5, 5, 6, 6, 7, 7)
RECV_RING = ((0, 12), (12, 12), (24, 6), (30, 6), (36, 6), (42, 6), (48, 6), (54, 6))
SEND_RING = ((0, 12), (12, 6), (18, 12))
N_RECV, N_SEND = 60, 30
LAG_A, LAG_B, LAG_C, LAG_D, LAG_E, LAG_F, LAG_G, LAG_H, LAG_M = -EARLY, 0, 2, 4, 6, 8, 10, 12, 14


def dot_nt(left, right):
    return lax.dot_general(left, right, (((1,), (1,)), ((), ())), preferred_element_type=F32)


def kernel(
    tok_hbm, grd_hbm, up_hbm, down_hbm, bias_hbm, relu_hbm, drop_hbm,
    gt_out, gu_out, gd_out, gb_out,
    tok, grd, tok_t, up, down, keep, acc, cols,
    part, r1, r2, summed, t1, t2, full,
    gtp, gtr, z1, z2, words, dropped, swapped, bias,
    ss, rs, ag_s, ag_r, gt_s, gt_r, sw_s, sw_r, loc,
):
    row = lax.axis_index("row")
    col = lax.axis_index("col")
    x, y, z, c = row // 4, row % 4, col // 2, col % 2

    def plus(v):
        return lax.rem(v + 1, 4)

    def minus(v):
        return lax.rem(v + 3, 4)

    def far(v):
        return lax.rem(v + 2, 4)

    xp, xm = (plus(x) * 4 + y, col), (minus(x) * 4 + y, col)
    yp, ym = (x * 4 + plus(y), col), (x * 4 + minus(y), col)
    zp, zm = (row, plus(z) * 2 + c), (row, minus(z) * 2 + c)
    sib = (row, z * 2 + (1 - c))
    everyone = (xp, xm, yp, ym, zp, zm, sib)

    def remote(src, dst, s, r, dev):
        return pltpu.make_async_remote_copy(
            src_ref=src, dst_ref=dst, send_sem=s, recv_sem=r, device_id=dev, device_id_type=MESH
        )

    third = FB // 3
    loads = [
        pltpu.make_async_copy(grd_hbm, grd.at[pl.ds(pl.multiple_of(col * 128, 128), 128)], loc.at[0]),
        pltpu.make_async_copy(down_hbm.at[pl.ds(0, third)], down.at[pl.ds(0, third)], loc.at[1]),
        pltpu.make_async_copy(down_hbm.at[pl.ds(third, 2 * third)], down.at[pl.ds(third, 2 * third)], loc.at[2]),
        pltpu.make_async_copy(tok_hbm, tok.at[pl.ds(pl.multiple_of(col * 128, 128), 128)], loc.at[3]),
        pltpu.make_async_copy(up_hbm, up, loc.at[4]),
        pltpu.make_async_copy(relu_hbm, words, loc.at[5]),
        pltpu.make_async_copy(drop_hbm, dropped, loc.at[6]),
        pltpu.make_async_copy(bias_hbm, bias, loc.at[7]),
    ]
    for k in (0, 1, 5, 6):
        loads[k].start()

    barrier = pltpu.get_barrier_semaphore()
    for dev in everyone:
        pl.semaphore_signal(barrier, inc=1, device_id=dev, device_id_type=MESH)
    mirror = (y * 4 + x, col)

    @pl.when(x != y)
    def _():
        pl.semaphore_signal(barrier, inc=1, device_id=mirror, device_id_type=MESH)

    pl.semaphore_wait(barrier, len(everyone) + (x != y).astype(jnp.int32))

    def block_at(buf, zz, cc, lo=0, n=128):
        return buf.at[pl.ds(pl.multiple_of((zz * 2 + cc) * 128 + lo, 64), n)]

    def gather_copies(a, src, buf):
        s, r = ag_s.at[a], ag_r.at[a]
        mine = block_at(buf, z, c)
        below, above, opp = minus(z), plus(z), far(z)
        lower, upper = block_at(buf, z, c, 0, 64), block_at(buf, z, c, 64, 64)
        src_lower, src_upper = src.at[pl.ds(0, 64)], src.at[pl.ds(64, 64)]
        far_lower, far_upper = block_at(buf, opp, c, 0, 64), block_at(buf, opp, c, 64, 64)
        sends = [
            (src_lower, lower, zp),
            (src_upper, upper, zp),
            (src_upper, upper, zm),
            (src_lower, lower, zm),
            (src, mine, sib),
            (block_at(buf, below, c, 0, 64), block_at(buf, below, c, 0, 64), zp),
            (block_at(buf, above, c, 64, 64), block_at(buf, above, c, 64, 64), zm),
            (block_at(buf, below, c), block_at(buf, below, c), sib),
            (block_at(buf, above, c), block_at(buf, above, c), sib),
            (far_lower, far_lower, sib),
            (far_upper, far_upper, sib),
        ]
        o = 1 - c
        lands = [
            block_at(buf, below, c, 0, 64), block_at(buf, below, c, 64, 64),
            block_at(buf, above, c, 64, 64), block_at(buf, above, c, 0, 64),
            block_at(buf, z, o),
            far_lower, far_upper,
            block_at(buf, below, o), block_at(buf, above, o),
            block_at(buf, opp, o, 0, 64), block_at(buf, opp, o, 64, 64),
        ]

        def send(k):
            a, b, dev = sends[k]
            return remote(a, b, s, r.at[k], dev)

        def recv(k):
            return remote(lands[k], lands[k], s, r.at[k], zp)

        return send, recv

    def all_sent(a, buf):
        size = buf.at[pl.ds(0, 896)]
        remote(size, size, ag_s.at[a], ag_r.at[a, 0], zp).wait_send()

    def gather_0(a, src, buf):
        send, _ = gather_copies(a, src, buf)
        for k in (4, 0, 2, 1, 3):
            send(k).start()

    def gather_1(a, src, buf):
        send, recv = gather_copies(a, src, buf)
        for got, on in ((0, 5), (2, 6), (1, 7), (3, 8)):
            recv(got).wait_recv()
            send(on).start()

    def gather_2(a, src, buf):
        send, recv = gather_copies(a, src, buf)
        for got, on in ((5, 9), (6, 10)):
            recv(got).wait_recv()
            send(on).start()

    def gather_3(a, src, buf):
        send, recv = gather_copies(a, src, buf)
        for k in (4, 7, 8, 9, 10):
            recv(k).wait_recv()
        all_sent(a, buf)

    gather_0(0, grd_hbm, grd)
    for k in (2, 7):
        loads[k].start()

    swap = remote(words, swapped, sw_s, sw_r, mirror)
    loads[5].wait()
    loads[6].wait()
    words[...] = words[...] & dropped[...]

    @pl.when(x != y)
    def _():
        swap.start()

    @pl.when(x == y)
    def _():
        swapped[...] = words[...]

    def unpack(j):
        word = lax.broadcasted_iota(jnp.int32, (FB // 16, HALF), 0)
        unit = lax.broadcasted_iota(jnp.int32, (FB // 16, HALF), 1)
        bit = lax.broadcasted_iota(jnp.int32, (64, HALF), 1) % 16
        for f, ref in enumerate((swapped, words)):
            got = ref[...]
            low = (got & 255).astype(F32).astype(BF)
            high = (got >> 8).astype(F32).astype(BF)
            spread = (word == (j * WIDE + f * HALF + unit) // 16).astype(F32).astype(BF)
            lows = jnp.dot(low, spread, preferred_element_type=F32).astype(jnp.int32)
            highs = jnp.dot(high, spread, preferred_element_type=F32).astype(jnp.int32)
            picked = jnp.where(bit < 8, lows, highs)
            on = (picked >> (bit % 8)) & 1
            keep[:, pl.ds(pl.multiple_of(j * WIDE + f * HALF, HALF), HALF)] = on.astype(F32) * KEEP

    flavours = ((x, y, xp, xm, yp, ym), (y, x, yp, ym, xp, xm))

    def send_sem(p, n):
        first, length = SEND_RING[n]
        return ss.at[first + lax.rem(p, length)]

    def recv_sem(p, n):
        first, length = RECV_RING[n]
        return rs.at[first + lax.rem(p, length)]

    def forward_block(p, left, weight, q):
        w = lax.rem(p, RING)
        res = weight(left[pl.ds(pl.multiple_of(q * 256, 256), 256), :]).astype(BF)
        for f in range(2):
            for k in range(4):
                part[w, f, k, q] = res[k * 64 : (k + 1) * 64, f * HALF : (f + 1) * HALF]

    def early(q, first, end):
        top = q // 2

        def one(p, carry):
            rows = down[pl.ds(pl.multiple_of(p * WIDE, WIDE), WIDE), :]
            forward_block(p, grd, lambda left: dot_nt(left, rows), q)
            for f in range(2):
                d1 = flavours[f][0]
                pt, ra, rb = part.at[p, f], r1.at[p, f], r2.at[p, f]

                def along(off):
                    to = lax.rem(d1 + off, 4)
                    return to, ((to * 4 + y, col) if f == 0 else (x * 4 + to, col))

                _, dev = along(1 + 2 * top)
                remote(pt.at[far(d1), q], ra.at[top, q - 2 * top], send_sem(p, 0), recv_sem(p, 0), dev).start()
                to, dev = along(3 - 2 * top)
                remote(pt.at[to, q], rb.at[1 - top, q], send_sem(p, 0), recv_sem(p, 1), dev).start()
            return carry

        lax.fori_loop(first, end, one, 0)

    loads[0].wait()
    loads[1].wait()

    def arrive(t, carry):
        send, recv = gather_copies(0, grd_hbm, grd)

        def forward_on(*pairs):
            for got, on in pairs:
                recv(got).wait_recv()
                send(on).start()

        @pl.when(t == 0)
        def _():
            recv(4).wait_recv()

        @pl.when(t == 1)
        def _():
            forward_on((0, 5), (2, 6))
            loads[2].wait()

        @pl.when(t == 2)
        def _():
            forward_on((1, 7), (3, 8))
            gather_0(1, tok_hbm, tok)
            loads[3].start()
            loads[4].start()
            recv(8).wait_recv()

        @pl.when(t == 3)
        def _():
            forward_on((5, 9), (6, 10))
            recv(7).wait_recv()

        @pl.when(t == 4)
        def _():
            for k in (9, 10):
                recv(k).wait_recv()

        u = (t * 4) // 5
        first = (t == 1).astype(jnp.int32) * (EARLY // 2)
        end = EARLY - (t == 0).astype(jnp.int32) * (EARLY - EARLY // 2)
        early(lax.rem(z + u + u // 2 - 2 * (u // 3), 4), first, end)
        return carry

    lax.fori_loop(0, 5, arrive, 0)
    all_sent(0, grd)
    loads[7].wait()

    def piece(p, f):
        d1, d2, p1, m1, p2, m2 = flavours[f]
        w, v = lax.rem(p, RING), lax.rem(p, HELD)
        pt, sm, g = part.at[w, f], summed.at[w, f], full.at[v, f]
        ra, rb, ta, tb = r1.at[w, f], r2.at[w, f], t1.at[w, f], t2.at[w, f]
        lo, hi = pl.ds(0, 2), pl.ds(2, 2)
        lo3, hi3 = pl.ds(0, 32), pl.ds(32, 32)
        n1, b1, o1 = plus(d1), minus(d1), far(d1)
        n2, b2, o2 = plus(d2), minus(d2), far(d2)
        sends = (
            (pt.at[o1, lo], ra.at[0], p1),
            (pt.at[o1, hi], ra.at[1], m1),
            (pt.at[n1, hi], rb.at[0, hi], p1),
            (pt.at[b1, lo], rb.at[1, lo], m1),
            (pt.at[n1, lo], rb.at[0, lo], p1),
            (pt.at[b1, hi], rb.at[1, hi], m1),
            (sm.at[o2, lo3], ta.at[0], p2),
            (sm.at[o2, hi3], ta.at[1], m2),
            (sm.at[n2, hi3], tb.at[0, hi3], p2),
            (sm.at[b2, lo3], tb.at[1, lo3], m2),
            (sm.at[n2, lo3], tb.at[0, lo3], p2),
            (sm.at[b2, hi3], tb.at[1, hi3], m2),
            (g.at[d1, d2], g.at[d1, d2], p2),
            (g.at[d1, d2], g.at[d1, d2], m2),
            (g.at[d1, b2, lo3], g.at[d1, b2, lo3], p2),
            (g.at[d1, n2, hi3], g.at[d1, n2, hi3], m2),
            (g.at[d1], g.at[d1], p1),
            (g.at[d1], g.at[d1], m1),
            (g.at[b1, lo], g.at[b1, lo], p1),
            (g.at[n1, hi], g.at[n1, hi], m1),
        )

        def start(*ks):
            for k in ks:
                a, b, dev = sends[k]
                remote(a, b, send_sem(p, min(k // 6, 2)), recv_sem(p, GROUP[k]), dev).start()

        return start

    def landed(p, n):
        w, v = lax.rem(p, RING), lax.rem(p, HELD)
        g = full.at[v, 0]
        size = (r1.at[w], r2.at[w], t1.at[w], t2.at[w], g.at[0], g.at[0, pl.ds(0, 2)], g, g.at[pl.ds(0, 2)])[n]
        remote(size, size, send_sem(p, 0), recv_sem(p, n), xp).wait_recv()

    def sent(p, n):
        size = grd.at[pl.ds(0, (256, 64, 320)[n])]
        remote(size, size, send_sem(p, n), recv_sem(p, 0), xp).wait_send()

    def when_piece(i, lag):
        p = i - lag
        return p, (p >= 0) & (p < NP)

    def forward(p, left, weight):
        for q in range(4):
            forward_block(p, left, weight, q)

    def stage_a(p):

        @pl.when(p < NJ)
        def _():
            rows = down[pl.ds(pl.multiple_of(p * WIDE, WIDE), WIDE), :]
            forward(p, grd, lambda left: dot_nt(left, rows))

        @pl.when(p >= NJ)
        def _():
            lanes = up[:, pl.ds(pl.multiple_of((p - NJ) * WIDE, WIDE), WIDE)]
            forward(p, tok, lambda left: jnp.dot(left, lanes, preferred_element_type=F32))

        for f in range(2):
            start = piece(p, f)
            start(0, 1, 2, 3)

    def stage_b(p):
        w = lax.rem(p, RING)
        landed(p, 0)
        for f in range(2):
            d1 = flavours[f][0]
            start = piece(p, f)
            n1, b1 = plus(d1), minus(d1)
            part[w, f, n1, 0:2] = (part[w, f, n1, 0:2].astype(F32) + r1[w, f, 0].astype(F32)).astype(BF)
            part[w, f, b1, 2:4] = (part[w, f, b1, 2:4].astype(F32) + r1[w, f, 1].astype(F32)).astype(BF)
            start(4, 5)

    def stage_c(p):
        w = lax.rem(p, RING)
        landed(p, 1)
        for f in range(2):
            d1 = flavours[f][0]
            start = piece(p, f)
            total = part[w, f, d1].astype(F32) + r2[w, f, 0].astype(F32) + r2[w, f, 1].astype(F32)
            summed[w, f] = total.astype(BF)
            start(6, 7, 8, 9)

    def stage_d(p):
        w = lax.rem(p, RING)
        landed(p, 2)
        sent(p, 0)
        for f in range(2):
            d2 = flavours[f][1]
            start = piece(p, f)
            n2, b2 = plus(d2), minus(d2)
            summed[w, f, n2, 0:32] = (summed[w, f, n2, 0:32].astype(F32) + t1[w, f, 0].astype(F32)).astype(BF)
            summed[w, f, b2, 32:64] = (summed[w, f, b2, 32:64].astype(F32) + t1[w, f, 1].astype(F32)).astype(BF)
            start(10, 11)

    def stage_e(p):
        w, v = lax.rem(p, RING), lax.rem(p, HELD)
        landed(p, 3)
        j = lax.rem(p, NJ)
        on_pre = (p >= NJ).astype(F32)
        for f in range(2):
            d1, d2 = flavours[f][:2]
            start = piece(p, f)
            total = summed[w, f, d2].astype(F32) + t2[w, f, 0].astype(F32) + t2[w, f, 1].astype(F32)
            lanes = pl.ds(pl.multiple_of(j * WIDE + f * HALF, HALF), HALF)
            total = total + bias[0:1, lanes] * on_pre
            full[v, f, d1, d2] = (keep[:, lanes] * total).astype(BF)
            start(12, 13)

    def stage_f(p):
        landed(p, 4)
        sent(p, 1)
        for f in range(2):
            start = piece(p, f)
            start(14, 15)

    def stage_g(p):
        landed(p, 5)
        for f in range(2):
            start = piece(p, f)
            start(16, 17)

    def stage_h(p):
        landed(p, 6)
        for f in range(2):
            start = piece(p, f)
            start(18, 19)

    def stage_m(p):
        w = lax.rem(p, HELD)
        landed(p, 7)
        for f in range(2):
            for q in range(4):
                for k in range(4):
                    cols[(q * 4 + k) * 64 : (q * 4 + k + 1) * 64, f * HALF : (f + 1) * HALF] = full[w, f, k, q]

        @pl.when(p < NJ)
        def _():
            j = p
            lanes = pl.ds(pl.multiple_of(j * WIDE, WIDE), WIDE)

            for q in range(3):
                res = jnp.dot(tok_t[q * 256 : (q + 1) * 256, :], cols[...], preferred_element_type=F32)
                gu_out[q * 256 : (q + 1) * 256, lanes] = (res * SCALE).astype(BF)
            gb_out[0:1, lanes] = jnp.sum(cols[...].astype(F32), axis=0, keepdims=True) * SCALE
            for q in range(4):
                acc[q * 256 : (q + 1) * 256, :] += dot_nt(cols[q * 256 : (q + 1) * 256, :], up[:, lanes])

        @pl.when(p >= NJ)
        def _():
            j = p - NJ

            res = lax.dot_general(cols[...], grd[...], (((0,), (0,)), ((), ())), preferred_element_type=F32)
            gd_out[pl.ds(pl.multiple_of(j * WIDE, WIDE), WIDE), :] = (res * SCALE).astype(BF)

        sent(p, 2)

    def gt_copies():
        s, r = gt_s, gt_r
        mine = gtp.at[c]
        above, below, opp = plus(z), minus(z), far(z)
        lo, hi = pl.ds(0, 64), pl.ds(64, 64)
        sends = [
            (gtp.at[1 - c], gtr, sib),
            (mine.at[opp, lo], z1.at[0], zp),
            (mine.at[opp, hi], z1.at[1], zm),
            (mine.at[above, hi], z2.at[0, hi], zp),
            (mine.at[below, lo], z2.at[1, lo], zm),
            (mine.at[above, lo], z2.at[0, lo], zp),
            (mine.at[below, hi], z2.at[1, hi], zm),
        ]

        def send(k):
            a, b, dev = sends[k]
            return remote(a, b, s, r.at[k], dev)

        return send

    def gt_0():
        for q in range(8):
            gtp[q % 2, q // 2] = acc[q * 128 : (q + 1) * 128, :].astype(BF)
        gt_copies()(0).start()

    def gt_1():
        send = gt_copies()
        send(0).wait_recv()
        for q in range(4):
            gtp[c, q] = (gtp[c, q].astype(F32) + gtr[q].astype(F32)).astype(BF)
        for k in (1, 2, 3, 4):
            send(k).start()

    def gt_2():
        send = gt_copies()
        send(1).wait_recv()
        send(2).wait_recv()
        above, below = plus(z), minus(z)
        gtp[c, above, 0:64] = (gtp[c, above, 0:64].astype(F32) + z1[0].astype(F32)).astype(BF)
        gtp[c, below, 64:128] = (gtp[c, below, 64:128].astype(F32) + z1[1].astype(F32)).astype(BF)
        send(5).start()
        send(6).start()

    def gt_3():
        send = gt_copies()
        for k in (3, 4, 5, 6):
            send(k).wait_recv()
        gt_out[...] = (gtp[c, z].astype(F32) + z2[0].astype(F32) + z2[1].astype(F32)).astype(BF)
        size = tok.at[pl.ds(0, 896)]
        remote(size, size, gt_s, gt_r.at[0], sib).wait_send()

    def step(i, carry):
        for fn, lag in (
            (stage_h, LAG_H), (stage_g, LAG_G), (stage_f, LAG_F), (stage_e, LAG_E),
            (stage_d, LAG_D), (stage_c, LAG_C), (stage_b, LAG_B), (stage_a, LAG_A), (stage_m, LAG_M),
        ):
            p, on = when_piece(i, lag)
            on = on & (p >= EARLY) if fn is stage_a else on
            pl.when(on)(functools.partial(fn, p))

        def at(n):
            return pl.when(i == n)

        @pl.when((i == 0) & (x != y))
        def _():
            swap.wait()

        pl.when(i < NJ)(functools.partial(unpack, i))

        @at(0)
        def _():
            gather_1(1, tok_hbm, tok)
            acc[...] = jnp.zeros_like(acc)

        @at(2)
        def _():
            gather_2(1, tok_hbm, tok)
            loads[3].wait()
            loads[4].wait()

        @at(3)
        def _():
            gather_3(1, tok_hbm, tok)

        @at(6)
        def _():
            for q in range(8):
                tok_t[:, q * 128 : (q + 1) * 128] = tok[q * 128 : (q + 1) * 128, :].T

        last = LAG_M + NJ - 1
        at(last)(gt_0)
        at(last + 2)(gt_1)
        at(last + 4)(gt_2)
        at(last + 7)(gt_3)
        return carry

    lax.fori_loop(0, NP + LAG_M, step, 0)


def flush(gt, gu, gd, gb, gt_out, gu_out, gd_out, gb_out, sem):
    copies = [pltpu.make_async_copy(gt, gt_out, sem.at[0]), pltpu.make_async_copy(gb, gb_out, sem.at[1])]
    for q in range(4):
        rows = pl.ds(q * DB // 4, DB // 4)
        copies.append(pltpu.make_async_copy(gu.at[rows], gu_out.at[rows], sem.at[2 + q]))
        rows = pl.ds(q * FB // 4, FB // 4)
        copies.append(pltpu.make_async_copy(gd.at[rows], gd_out.at[rows], sem.at[6 + q]))
    for cp in copies:
        cp.start()
    for cp in copies:
        cp.wait()


def body(tokens, grad_out, up_weight, down_weight, up_bias, relu_bits, drop_bits):
    hbm = pl.BlockSpec(memory_space=pl.ANY)
    vmem = pl.BlockSpec(memory_space=pltpu.VMEM)
    dma = pltpu.SemaphoreType.DMA
    shapes = (((128, DB), BF), ((DB, FB), BF), ((FB, DB), BF), ((1, FB), F32))
    held = pl.pallas_call(
        kernel,
        out_shape=tuple(pltpu.VMEM(shape, dtype) for shape, dtype in shapes),
        in_specs=[hbm] * 7,
        out_specs=(vmem,) * 4,
        scratch_shapes=[
            pltpu.VMEM((TOK, DB), BF),
            pltpu.VMEM((TOK, DB), BF),
            pltpu.VMEM((DB, TOK), BF),
            pltpu.VMEM((DB, FB), BF),
            pltpu.VMEM((FB, DB), BF),
            pltpu.VMEM((64, FB), F32),
            pltpu.VMEM((TOK, DB), F32),
            pltpu.VMEM((TOK, WIDE), BF),
            pltpu.VMEM((RING, 2, 4, 4, 64, HALF), BF),
            pltpu.VMEM((RING, 2, 2, 2, 64, HALF), BF),
            pltpu.VMEM((RING, 2, 2, 4, 64, HALF), BF),
            pltpu.VMEM((RING, 2, 4, 64, HALF), BF),
            pltpu.VMEM((RING, 2, 2, 32, HALF), BF),
            pltpu.VMEM((RING, 2, 2, 64, HALF), BF),
            pltpu.VMEM((HELD, 2, 4, 4, 64, HALF), BF),
            pltpu.VMEM((2, 4, 128, DB), BF),
            pltpu.VMEM((4, 128, DB), BF),
            pltpu.VMEM((2, 64, DB), BF),
            pltpu.VMEM((2, 128, DB), BF),
            pltpu.VMEM((64, FB // 16), jnp.int32),
            pltpu.VMEM((64, FB // 16), jnp.int32),
            pltpu.VMEM((64, FB // 16), jnp.int32),
            pltpu.VMEM((1, FB), F32),
            dma((N_SEND,)),
            dma((N_RECV,)),
            dma((2,)),
            dma((2, 11)),
            dma,
            dma((7,)),
            dma,
            dma,
            dma((8,)),
        ],
        compiler_params=pltpu.CompilerParams(
            collective_id=0, has_side_effects=True, vmem_limit_bytes=48 * 2**20
        ),
        cost_estimate=pl.CostEstimate(
            flops=10 * TOK * DB * FB, bytes_accessed=10 * DB * FB, transcendentals=0
        ),
        name="fused",
    )(tokens, grad_out, up_weight, down_weight, up_bias.reshape(1, FB), relu_bits, drop_bits)
    gt, gu, gd, gb = pl.pallas_call(
        flush,
        out_shape=tuple(jax.ShapeDtypeStruct(shape, dtype) for shape, dtype in shapes),
        in_specs=[vmem] * 4,
        out_specs=(hbm,) * 4,
        scratch_shapes=[dma((10,))],
        compiler_params=pltpu.CompilerParams(vmem_limit_bytes=2**20),
        name="flush",
    )(*held)
    return gt, gu, gd, gb.reshape(FB)


def solution(mesh):
    return jax.shard_map(
        body,
        mesh=mesh,
        in_specs=(
            P("col", "row"), P("col", "row"), P("row", "col"), P("col", "row"),
            P("col"), P("row", "col"), P("row", "col"),
        ),
        out_specs=(P("col", "row"), P("row", "col"), P("col", "row"), P("col")),
        check_vma=False,
    )
```

```python
import functools
import math

import jax
import jax.numpy as jnp
from jax import lax
from jax.experimental import pallas as pl
from jax.experimental.pallas import tpu as pltpu
from jax.sharding import PartitionSpec as P

MESH = pl.DeviceIdType.MESH
TOK = 1024
DB = 768
FB = 3072
WIDE = 256
HALF = 128
NJ = FB // WIDE
NP = 2 * NJ
RING = 16
HELD = 16
EARLY = 8
LATE = 2
KEEP = 1.0 / 0.9
SCALE = 1.0 / math.sqrt(TOK)
BF = jnp.bfloat16
F32 = jnp.float32
GROUP = (0, 0, 1, 1, 1, 1, 2, 2, 3, 3, 3, 3, 4, 4, 5, 5, 6, 6, 7, 7, 7)
RECV_RING = ((0, 12), (12, 12), (24, 6), (30, 6), (36, 6), (42, 6), (48, 6), (54, 12))
SEND_RING = ((0, 12), (12, 6), (18, 12))
N_RECV, N_SEND = 66, 30
LAG_A, LAG_B, LAG_C, LAG_D, LAG_E, LAG_F, LAG_G, LAG_H, LAG_M = -EARLY, 0, 2, 4, 6, 8, 10, 12, 14


def dot_nt(left, right):
    return lax.dot_general(left, right, (((1,), (1,)), ((), ())), preferred_element_type=F32)


def kernel(
    tok_hbm, grd_hbm, up_hbm, down_hbm, bias_hbm, relu_hbm, drop_hbm,
    gt_out, gu_out, gd_out, gb_out, late, grd,
    tok, tok_t, up, down, keep, acc, cols,
    part, r1, r2, summed, t1, t2, full,
    gtp, gtr, z1, z2, words, dropped, swapped, bias,
    ss, rs, ag_s, ag_r, gt_s, gt_r, sw_s, sw_r, loc,
):
    row = lax.axis_index("row")
    col = lax.axis_index("col")
    x, y, z, c = row // 4, row % 4, col // 2, col % 2

    def plus(v):
        return lax.rem(v + 1, 4)

    def minus(v):
        return lax.rem(v + 3, 4)

    def far(v):
        return lax.rem(v + 2, 4)

    xp, xm = (plus(x) * 4 + y, col), (minus(x) * 4 + y, col)
    yp, ym = (x * 4 + plus(y), col), (x * 4 + minus(y), col)
    zp, zm = (row, plus(z) * 2 + c), (row, minus(z) * 2 + c)
    sib = (row, z * 2 + (1 - c))
    xf, yf = (far(x) * 4 + y, col), (x * 4 + far(y), col)
    everyone = (xp, xm, yp, ym, zp, zm, sib, xf, yf)

    def remote(src, dst, s, r, dev):
        return pltpu.make_async_remote_copy(
            src_ref=src, dst_ref=dst, send_sem=s, recv_sem=r, device_id=dev, device_id_type=MESH
        )

    third = FB // 3
    loads = [
        pltpu.make_async_copy(grd_hbm, grd.at[pl.ds(pl.multiple_of(col * 128, 128), 128)], loc.at[0]),
        pltpu.make_async_copy(down_hbm.at[pl.ds(0, third)], down.at[pl.ds(0, third)], loc.at[1]),
        pltpu.make_async_copy(down_hbm.at[pl.ds(third, 2 * third)], down.at[pl.ds(third, 2 * third)], loc.at[2]),
        pltpu.make_async_copy(tok_hbm, tok.at[pl.ds(pl.multiple_of(col * 128, 128), 128)], loc.at[3]),
        pltpu.make_async_copy(up_hbm, up, loc.at[4]),
        pltpu.make_async_copy(relu_hbm, words, loc.at[5]),
        pltpu.make_async_copy(drop_hbm, dropped, loc.at[6]),
        pltpu.make_async_copy(bias_hbm, bias, loc.at[7]),
    ]
    for k in (0, 1, 5, 6):
        loads[k].start()

    barrier = pltpu.get_barrier_semaphore()
    for dev in everyone:
        pl.semaphore_signal(barrier, inc=1, device_id=dev, device_id_type=MESH)
    mirror = (y * 4 + x, col)

    @pl.when(x != y)
    def _():
        pl.semaphore_signal(barrier, inc=1, device_id=mirror, device_id_type=MESH)

    pl.semaphore_wait(barrier, len(everyone) + (x != y).astype(jnp.int32))

    def block_at(buf, zz, cc, lo=0, n=128):
        return buf.at[pl.ds(pl.multiple_of((zz * 2 + cc) * 128 + lo, 64), n)]

    def gather_copies(a, src, buf):
        s, r = ag_s.at[a], ag_r.at[a]
        mine = block_at(buf, z, c)
        below, above, opp = minus(z), plus(z), far(z)
        lower, upper = block_at(buf, z, c, 0, 64), block_at(buf, z, c, 64, 64)
        src_lower, src_upper = src.at[pl.ds(0, 64)], src.at[pl.ds(64, 64)]
        far_lower, far_upper = block_at(buf, opp, c, 0, 64), block_at(buf, opp, c, 64, 64)
        sends = [
            (src_lower, lower, zp),
            (src_upper, upper, zp),
            (src_upper, upper, zm),
            (src_lower, lower, zm),
            (src, mine, sib),
            (block_at(buf, below, c, 0, 64), block_at(buf, below, c, 0, 64), zp),
            (block_at(buf, above, c, 64, 64), block_at(buf, above, c, 64, 64), zm),
            (block_at(buf, below, c), block_at(buf, below, c), sib),
            (block_at(buf, above, c), block_at(buf, above, c), sib),
            (far_lower, far_lower, sib),
            (far_upper, far_upper, sib),
        ]
        o = 1 - c
        lands = [
            block_at(buf, below, c, 0, 64), block_at(buf, below, c, 64, 64),
            block_at(buf, above, c, 64, 64), block_at(buf, above, c, 0, 64),
            block_at(buf, z, o),
            far_lower, far_upper,
            block_at(buf, below, o), block_at(buf, above, o),
            block_at(buf, opp, o, 0, 64), block_at(buf, opp, o, 64, 64),
        ]

        def send(k):
            a, b, dev = sends[k]
            return remote(a, b, s, r.at[k], dev)

        def recv(k):
            return remote(lands[k], lands[k], s, r.at[k], zp)

        return send, recv

    def all_sent(a, buf):
        size = buf.at[pl.ds(0, 896)]
        remote(size, size, ag_s.at[a], ag_r.at[a, 0], zp).wait_send()

    def gather_0(a, src, buf):
        send, _ = gather_copies(a, src, buf)
        for k in (4, 0, 2, 1, 3):
            send(k).start()

    def gather_1(a, src, buf):
        send, recv = gather_copies(a, src, buf)
        for got, on in ((0, 5), (2, 6), (1, 7), (3, 8)):
            recv(got).wait_recv()
            send(on).start()

    def gather_2(a, src, buf):
        send, recv = gather_copies(a, src, buf)
        for got, on in ((5, 9), (6, 10)):
            recv(got).wait_recv()
            send(on).start()

    def gather_3(a, src, buf):
        send, recv = gather_copies(a, src, buf)
        for k in (4, 7, 8, 9, 10):
            recv(k).wait_recv()
        all_sent(a, buf)

    gather_0(0, grd_hbm, grd)
    for k in (2, 7):
        loads[k].start()

    swap = remote(words, swapped, sw_s, sw_r, mirror)
    loads[5].wait()
    loads[6].wait()
    words[...] = words[...] & dropped[...]

    @pl.when(x != y)
    def _():
        swap.start()

    @pl.when(x == y)
    def _():
        swapped[...] = words[...]

    def unpack(j):
        word = lax.broadcasted_iota(jnp.int32, (FB // 16, HALF), 0)
        unit = lax.broadcasted_iota(jnp.int32, (FB // 16, HALF), 1)
        bit = lax.broadcasted_iota(jnp.int32, (64, HALF), 1) % 16
        for f, ref in enumerate((swapped, words)):
            got = ref[...]
            low = (got & 255).astype(F32).astype(BF)
            high = (got >> 8).astype(F32).astype(BF)
            spread = (word == (j * WIDE + f * HALF + unit) // 16).astype(F32).astype(BF)
            lows = jnp.dot(low, spread, preferred_element_type=F32).astype(jnp.int32)
            highs = jnp.dot(high, spread, preferred_element_type=F32).astype(jnp.int32)
            picked = jnp.where(bit < 8, lows, highs)
            on = (picked >> (bit % 8)) & 1
            keep[:, pl.ds(pl.multiple_of(j * WIDE + f * HALF, HALF), HALF)] = on.astype(F32) * KEEP

    flavours = ((x, y, xp, xm, yp, ym, xf), (y, x, yp, ym, xp, xm, yf))

    def send_sem(p, n):
        first, length = SEND_RING[n]
        return ss.at[first + lax.rem(p, length)]

    def recv_sem(p, n):
        first, length = RECV_RING[n]
        return rs.at[first + lax.rem(p, length)]

    def forward_block(p, left, weight, q):
        w = lax.rem(p, RING)
        res = weight(left[pl.ds(pl.multiple_of(q * 256, 256), 256), :]).astype(BF)
        for f in range(2):
            for k in range(4):
                part[w, f, k, q] = res[k * 64 : (k + 1) * 64, f * HALF : (f + 1) * HALF]

    def early(q, first, end):
        top = q // 2

        def one(p, carry):
            rows = down[pl.ds(pl.multiple_of(p * WIDE, WIDE), WIDE), :]
            forward_block(p, grd, lambda left: dot_nt(left, rows), q)
            for f in range(2):
                d1 = flavours[f][0]
                pt, ra, rb = part.at[p, f], r1.at[p, f], r2.at[p, f]

                def along(off):
                    to = lax.rem(d1 + off, 4)
                    return to, ((to * 4 + y, col) if f == 0 else (x * 4 + to, col))

                _, dev = along(1 + 2 * top)
                remote(pt.at[far(d1), q], ra.at[top, q - 2 * top], send_sem(p, 0), recv_sem(p, 0), dev).start()
                to, dev = along(3 - 2 * top)
                remote(pt.at[to, q], rb.at[1 - top, q], send_sem(p, 0), recv_sem(p, 1), dev).start()
            return carry

        lax.fori_loop(first, end, one, 0)

    loads[0].wait()
    loads[1].wait()

    def arrive(t, carry):
        send, recv = gather_copies(0, grd_hbm, grd)

        def forward_on(*pairs):
            for got, on in pairs:
                recv(got).wait_recv()
                send(on).start()

        @pl.when(t == 0)
        def _():
            recv(4).wait_recv()

        @pl.when(t == 1)
        def _():
            forward_on((0, 5), (2, 6))
            loads[2].wait()

        @pl.when(t == 2)
        def _():
            forward_on((1, 7), (3, 8))
            gather_0(1, tok_hbm, tok)
            loads[3].start()
            loads[4].start()
            recv(8).wait_recv()

        @pl.when(t == 3)
        def _():
            forward_on((5, 9), (6, 10))
            recv(7).wait_recv()

        @pl.when(t == 4)
        def _():
            for k in (9, 10):
                recv(k).wait_recv()

        u = (t * 4) // 5
        first = (t == 1).astype(jnp.int32) * (EARLY // 2)
        end = EARLY + (t == 1).astype(jnp.int32) * (NJ - EARLY) - (t == 0).astype(jnp.int32) * (EARLY - EARLY // 2)
        early(lax.rem(z + u + u // 2 - 2 * (u // 3), 4), first, end)
        return carry

    lax.fori_loop(0, 5, arrive, 0)
    all_sent(0, grd)
    loads[7].wait()

    def piece(p, f):
        d1, d2, p1, m1, p2, m2, f1 = flavours[f]
        w, v = lax.rem(p, RING), lax.rem(p, HELD)
        pt, sm, g = part.at[w, f], summed.at[w, f], full.at[v, f]
        ra, rb, ta, tb = r1.at[w, f], r2.at[w, f], t1.at[w, f], t2.at[w, f]
        lo, hi = pl.ds(0, 2), pl.ds(2, 2)
        lo3, hi3 = pl.ds(0, 32), pl.ds(32, 32)
        n1, b1, o1 = plus(d1), minus(d1), far(d1)
        n2, b2, o2 = plus(d2), minus(d2), far(d2)
        sends = (
            (pt.at[o1, lo], ra.at[0], p1),
            (pt.at[o1, hi], ra.at[1], m1),
            (pt.at[n1, hi], rb.at[0, hi], p1),
            (pt.at[b1, lo], rb.at[1, lo], m1),
            (pt.at[n1, lo], rb.at[0, lo], p1),
            (pt.at[b1, hi], rb.at[1, hi], m1),
            (sm.at[o2, lo3], ta.at[0], p2),
            (sm.at[o2, hi3], ta.at[1], m2),
            (sm.at[n2, hi3], tb.at[0, hi3], p2),
            (sm.at[b2, lo3], tb.at[1, lo3], m2),
            (sm.at[n2, lo3], tb.at[0, lo3], p2),
            (sm.at[b2, hi3], tb.at[1, hi3], m2),
            (g.at[d1, d2], g.at[d1, d2], p2),
            (g.at[d1, d2], g.at[d1, d2], m2),
            (g.at[d1, b2, lo3], g.at[d1, b2, lo3], p2),
            (g.at[d1, n2, hi3], g.at[d1, n2, hi3], m2),
            (g.at[d1], g.at[d1], p1),
            (g.at[d1], g.at[d1], m1),
            (g.at[b1, lo], g.at[b1, lo], p1),
            (g.at[n1, hi], g.at[n1, hi], m1),
            (g.at[d1], g.at[d1], f1),
        )

        def start(*ks):
            for k in ks:
                a, b, dev = sends[k]
                remote(a, b, send_sem(p, min(k // 6, 2)), recv_sem(p, GROUP[k]), dev).start()

        return start

    def landed(p, n):
        w, v = lax.rem(p, RING), lax.rem(p, HELD)
        g = full.at[v, 0]
        size = (r1.at[w], r2.at[w], t1.at[w], t2.at[w], g.at[0], g.at[0, pl.ds(0, 2)], g, g.at[pl.ds(0, 2)])[n]
        remote(size, size, send_sem(p, 0), recv_sem(p, n), xp).wait_recv()

    def sent(p, n):
        size = grd.at[pl.ds(0, (256, 64, 320)[n])]
        remote(size, size, send_sem(p, n), recv_sem(p, 0), xp).wait_send()

    def when_piece(i, lag):
        p = i - lag
        return p, (p >= 0) & (p < NP)

    def stage_a(p):
        @pl.when(p < NJ)
        def _():
            def other(n, carry):
                early(lax.rem(z + n, 4), p, p + 1)
                return carry

            lax.fori_loop(1, 4, other, 0)

        @pl.when(p >= NJ)
        def _():
            lanes = up[:, pl.ds(pl.multiple_of((p - NJ) * WIDE, WIDE), WIDE)]
            for q in range(4):
                forward_block(p, tok, lambda left: jnp.dot(left, lanes, preferred_element_type=F32), q)
            for f in range(2):
                start = piece(p, f)
                start(0, 1, 2, 3)

    def stage_b(p):
        w = lax.rem(p, RING)
        landed(p, 0)
        for f in range(2):
            d1 = flavours[f][0]
            start = piece(p, f)
            n1, b1 = plus(d1), minus(d1)
            part[w, f, n1, 0:2] = (part[w, f, n1, 0:2].astype(F32) + r1[w, f, 0].astype(F32)).astype(BF)
            part[w, f, b1, 2:4] = (part[w, f, b1, 2:4].astype(F32) + r1[w, f, 1].astype(F32)).astype(BF)
            start(4, 5)

    def stage_c(p):
        w = lax.rem(p, RING)
        landed(p, 1)
        for f in range(2):
            d1 = flavours[f][0]
            start = piece(p, f)
            total = part[w, f, d1].astype(F32) + r2[w, f, 0].astype(F32) + r2[w, f, 1].astype(F32)
            summed[w, f] = total.astype(BF)
            start(6, 7, 8, 9)

    def stage_d(p):
        w = lax.rem(p, RING)
        landed(p, 2)
        sent(p, 0)
        for f in range(2):
            d2 = flavours[f][1]
            start = piece(p, f)
            n2, b2 = plus(d2), minus(d2)
            summed[w, f, n2, 0:32] = (summed[w, f, n2, 0:32].astype(F32) + t1[w, f, 0].astype(F32)).astype(BF)
            summed[w, f, b2, 32:64] = (summed[w, f, b2, 32:64].astype(F32) + t1[w, f, 1].astype(F32)).astype(BF)
            start(10, 11)

    def stage_e(p):
        w, v = lax.rem(p, RING), lax.rem(p, HELD)
        landed(p, 3)
        j = lax.rem(p, NJ)
        on_pre = (p >= NJ).astype(F32)
        for f in range(2):
            d1, d2 = flavours[f][:2]
            start = piece(p, f)
            total = summed[w, f, d2].astype(F32) + t2[w, f, 0].astype(F32) + t2[w, f, 1].astype(F32)
            lanes = pl.ds(pl.multiple_of(j * WIDE + f * HALF, HALF), HALF)
            total = total + bias[0:1, lanes] * on_pre
            full[v, f, d1, d2] = (keep[:, lanes] * total).astype(BF)
            start(12, 13)

    def stage_f(p):
        landed(p, 4)
        sent(p, 1)
        for f in range(2):
            start = piece(p, f)
            start(14, 15)

    def stage_g(p):
        landed(p, 5)
        for f in range(2):
            start = piece(p, f)
            start(16, 17)
            pl.when(p >= NP - LATE)(functools.partial(start, 20))

    def stage_h(p):
        landed(p, 6)
        for f in range(2):
            start = piece(p, f)
            pl.when(p < NP - LATE)(functools.partial(start, 18, 19))

    def collect(p, ref):
        w = lax.rem(p, HELD)
        landed(p, 7)
        for f in range(2):
            for q in range(4):
                for k in range(4):
                    ref[(q * 4 + k) * 64 : (q * 4 + k + 1) * 64, f * HALF : (f + 1) * HALF] = full[w, f, k, q]

    def stage_m(p):
        collect(p, cols)

        @pl.when(p < NJ)
        def _():
            j = p
            lanes = pl.ds(pl.multiple_of(j * WIDE, WIDE), WIDE)

            for q in range(3):
                res = jnp.dot(tok_t[q * 256 : (q + 1) * 256, :], cols[...], preferred_element_type=F32)
                gu_out[q * 256 : (q + 1) * 256, lanes] = (res * SCALE).astype(BF)
            gb_out[0:1, lanes] = jnp.sum(cols[...].astype(F32), axis=0, keepdims=True) * SCALE
            for q in range(4):
                acc[q * 256 : (q + 1) * 256, :] += dot_nt(cols[q * 256 : (q + 1) * 256, :], up[:, lanes])

        @pl.when(p >= NJ)
        def _():
            j = p - NJ

            res = lax.dot_general(cols[...], grd[...], (((0,), (0,)), ((), ())), preferred_element_type=F32)
            gd_out[pl.ds(pl.multiple_of(j * WIDE, WIDE), WIDE), :] = (res * SCALE).astype(BF)

        sent(p, 2)

    def gt_copies():
        s, r = gt_s, gt_r
        mine = gtp.at[c]
        above, below, opp = plus(z), minus(z), far(z)
        lo, hi = pl.ds(0, 64), pl.ds(64, 64)
        sends = [
            (gtp.at[1 - c], gtr, sib),
            (mine.at[opp, lo], z1.at[0], zp),
            (mine.at[opp, hi], z1.at[1], zm),
            (mine.at[above, hi], z2.at[0, hi], zp),
            (mine.at[below, lo], z2.at[1, lo], zm),
            (mine.at[above, lo], z2.at[0, lo], zp),
            (mine.at[below, hi], z2.at[1, hi], zm),
        ]

        def send(k):
            a, b, dev = sends[k]
            return remote(a, b, s, r.at[k], dev)

        return send

    def gt_0():
        for q in range(8):
            gtp[q % 2, q // 2] = acc[q * 128 : (q + 1) * 128, :].astype(BF)
        gt_copies()(0).start()

    def gt_1():
        send = gt_copies()
        send(0).wait_recv()
        for q in range(4):
            gtp[c, q] = (gtp[c, q].astype(F32) + gtr[q].astype(F32)).astype(BF)
        for k in (1, 2, 3, 4):
            send(k).start()

    def gt_2():
        send = gt_copies()
        send(1).wait_recv()
        send(2).wait_recv()
        above, below = plus(z), minus(z)
        gtp[c, above, 0:64] = (gtp[c, above, 0:64].astype(F32) + z1[0].astype(F32)).astype(BF)
        gtp[c, below, 64:128] = (gtp[c, below, 64:128].astype(F32) + z1[1].astype(F32)).astype(BF)
        send(5).start()
        send(6).start()

    def gt_3():
        send = gt_copies()
        for k in (3, 4, 5, 6):
            send(k).wait_recv()
        gt_out[...] = (gtp[c, z].astype(F32) + z2[0].astype(F32) + z2[1].astype(F32)).astype(BF)
        size = tok.at[pl.ds(0, 896)]
        remote(size, size, gt_s, gt_r.at[0], sib).wait_send()

    def step(i, carry):
        for fn, lag in (
            (stage_h, LAG_H), (stage_g, LAG_G), (stage_f, LAG_F), (stage_e, LAG_E),
            (stage_d, LAG_D), (stage_c, LAG_C), (stage_b, LAG_B), (stage_a, LAG_A), (stage_m, LAG_M),
        ):
            p, on = when_piece(i, lag)
            on = on & (p >= EARLY) if fn is stage_a else on
            pl.when(on)(functools.partial(fn, p))

        def at(n):
            return pl.when(i == n)

        @pl.when((i == 0) & (x != y))
        def _():
            swap.wait()

        pl.when((i >= 5) & (i < NJ + 5))(functools.partial(unpack, i - 5))

        @at(0)
        def _():
            gather_1(1, tok_hbm, tok)

        @at(2)
        def _():
            gather_2(1, tok_hbm, tok)
            loads[3].wait()
            loads[4].wait()

        @at(3)
        def _():
            gather_3(1, tok_hbm, tok)

        @at(12)
        def _():
            acc[...] = jnp.zeros_like(acc)
            for q in range(8):
                tok_t[:, q * 128 : (q + 1) * 128] = tok[q * 128 : (q + 1) * 128, :].T

        last = LAG_M + NJ - 1
        at(last)(gt_0)
        at(last + 2)(gt_1)
        at(last + 4)(gt_2)
        at(last + 7)(gt_3)
        return carry

    lax.fori_loop(0, NP + LAG_H, step, 0)
    for k in range(LATE):
        collect(NP - LATE + k, late.at[k])
        sent(NP - LATE + k, 2)


def flush(gt, gu, gd, gb, late, grd, gt_out, gu_out, gd_out, gb_out, rows, sem):
    done = FB - LATE * WIDE
    copies = [pltpu.make_async_copy(gt, gt_out, sem.at[0]), pltpu.make_async_copy(gb, gb_out, sem.at[1])]
    for q in range(4):
        part = pl.ds(q * DB // 4, DB // 4)
        copies.append(pltpu.make_async_copy(gu.at[part], gu_out.at[part], sem.at[2 + q]))
        part = pl.ds(q * done // 4, done // 4)
        copies.append(pltpu.make_async_copy(gd.at[part], gd_out.at[part], sem.at[6 + q]))
    for cp in copies:
        cp.start()
    for k in range(LATE):
        res = lax.dot_general(late[k], grd[...], (((0,), (0,)), ((), ())), preferred_element_type=F32)
        rows[k] = (res * SCALE).astype(BF)
        cp = pltpu.make_async_copy(rows.at[k], gd_out.at[pl.ds(done + k * WIDE, WIDE)], sem.at[10 + k])
        cp.start()
        copies.append(cp)
    for cp in copies:
        cp.wait()


def body(tokens, grad_out, up_weight, down_weight, up_bias, relu_bits, drop_bits):
    hbm = pl.BlockSpec(memory_space=pl.ANY)
    vmem = pl.BlockSpec(memory_space=pltpu.VMEM)
    dma = pltpu.SemaphoreType.DMA
    shapes = (((128, DB), BF), ((DB, FB), BF), ((FB, DB), BF), ((1, FB), F32))
    kept = (((LATE, TOK, WIDE), BF), ((TOK, DB), BF))
    held = pl.pallas_call(
        kernel,
        out_shape=tuple(pltpu.VMEM(shape, dtype) for shape, dtype in shapes + kept),
        in_specs=[hbm] * 7,
        out_specs=(vmem,) * 6,
        scratch_shapes=[
            pltpu.VMEM((TOK, DB), BF),
            pltpu.VMEM((DB, TOK), BF),
            pltpu.VMEM((DB, FB), BF),
            pltpu.VMEM((FB, DB), BF),
            pltpu.VMEM((64, FB), F32),
            pltpu.VMEM((TOK, DB), F32),
            pltpu.VMEM((TOK, WIDE), BF),
            pltpu.VMEM((RING, 2, 4, 4, 64, HALF), BF),
            pltpu.VMEM((RING, 2, 2, 2, 64, HALF), BF),
            pltpu.VMEM((RING, 2, 2, 4, 64, HALF), BF),
            pltpu.VMEM((RING, 2, 4, 64, HALF), BF),
            pltpu.VMEM((RING, 2, 2, 32, HALF), BF),
            pltpu.VMEM((RING, 2, 2, 64, HALF), BF),
            pltpu.VMEM((HELD, 2, 4, 4, 64, HALF), BF),
            pltpu.VMEM((2, 4, 128, DB), BF),
            pltpu.VMEM((4, 128, DB), BF),
            pltpu.VMEM((2, 64, DB), BF),
            pltpu.VMEM((2, 128, DB), BF),
            pltpu.VMEM((64, FB // 16), jnp.int32),
            pltpu.VMEM((64, FB // 16), jnp.int32),
            pltpu.VMEM((64, FB // 16), jnp.int32),
            pltpu.VMEM((1, FB), F32),
            dma((N_SEND,)),
            dma((N_RECV,)),
            dma((2,)),
            dma((2, 11)),
            dma,
            dma((7,)),
            dma,
            dma,
            dma((8,)),
        ],
        compiler_params=pltpu.CompilerParams(
            collective_id=0, has_side_effects=True, vmem_limit_bytes=48 * 2**20
        ),
        cost_estimate=pl.CostEstimate(
            flops=10 * TOK * DB * FB, bytes_accessed=10 * DB * FB, transcendentals=0
        ),
        name="fused",
    )(tokens, grad_out, up_weight, down_weight, up_bias.reshape(1, FB), relu_bits, drop_bits)
    gt, gu, gd, gb = pl.pallas_call(
        flush,
        out_shape=tuple(jax.ShapeDtypeStruct(shape, dtype) for shape, dtype in shapes),
        in_specs=[vmem] * 6,
        out_specs=(hbm,) * 4,
        scratch_shapes=[pltpu.VMEM((LATE, WIDE, DB), BF), dma((10 + LATE,))],
        compiler_params=pltpu.CompilerParams(vmem_limit_bytes=6 * 2**20),
        name="flush",
    )(*held)
    return gt, gu, gd, gb.reshape(FB)


def solution(mesh):
    return jax.shard_map(
        body,
        mesh=mesh,
        in_specs=(
            P("col", "row"), P("col", "row"), P("row", "col"), P("col", "row"),
            P("col"), P("row", "col"), P("row", "col"),
        ),
        out_specs=(P("col", "row"), P("row", "col"), P("col", "row"), P("col")),
        check_vma=False,
    )
```

```python
import functools
import math

import jax
import jax.numpy as jnp
from jax import lax
from jax.experimental import pallas as pl
from jax.experimental.pallas import tpu as pltpu
from jax.sharding import PartitionSpec as P

MESH = pl.DeviceIdType.MESH
TOK = 1024
DB = 768
FB = 3072
WIDE = 256
HALF = 128
NJ = FB // WIDE
NP = 2 * NJ
RING = 16
HELD = 16
EARLY = 8
LATE = 2
KEEP = 1.0 / 0.9
SCALE = 1.0 / math.sqrt(TOK)
BF = jnp.bfloat16
F32 = jnp.float32
GROUP = (0, 0, 1, 1, 1, 1, 2, 2, 3, 3, 3, 3, 4, 4, 5, 5, 6, 6, 7, 7, 7)
RECV_RING = ((0, 12), (12, 12), (24, 6), (30, 6), (36, 6), (42, 6), (48, 6), (54, 12))
SEND_RING = ((0, 12), (12, 6), (18, 12))
N_RECV, N_SEND = 66, 30
LAG_A, LAG_B, LAG_C, LAG_D, LAG_E, LAG_F, LAG_G, LAG_H, LAG_M = -EARLY, 0, 2, 4, 6, 8, 10, 12, 14


def dot_nt(left, right):
    return lax.dot_general(left, right, (((1,), (1,)), ((), ())), preferred_element_type=F32)


def kernel(
    tok_hbm, grd_hbm, up_hbm, down_hbm, bias_hbm, relu_hbm, drop_hbm,
    gt_out, gu_out, gd_out, gb_out, late, grd,
    tok, tok_t, up, down, keep, acc, cols,
    part, r1, r2, summed, t1, t2, full,
    gtp, gtr, z1, z2, words, dropped, swapped, bias,
    ss, rs, ag_s, ag_r, gt_s, gt_r, sw_s, sw_r, loc,
):
    row = lax.axis_index("row")
    col = lax.axis_index("col")
    x, y, z, c = row // 4, row % 4, col // 2, col % 2

    def plus(v):
        return lax.rem(v + 1, 4)

    def minus(v):
        return lax.rem(v + 3, 4)

    def far(v):
        return lax.rem(v + 2, 4)

    xp, xm = (plus(x) * 4 + y, col), (minus(x) * 4 + y, col)
    yp, ym = (x * 4 + plus(y), col), (x * 4 + minus(y), col)
    zp, zm = (row, plus(z) * 2 + c), (row, minus(z) * 2 + c)
    sib = (row, z * 2 + (1 - c))
    xf, yf = (far(x) * 4 + y, col), (x * 4 + far(y), col)
    everyone = (xp, xm, yp, ym, zp, zm, sib, xf, yf)

    def remote(src, dst, s, r, dev):
        return pltpu.make_async_remote_copy(
            src_ref=src, dst_ref=dst, send_sem=s, recv_sem=r, device_id=dev, device_id_type=MESH
        )

    third = FB // 3
    loads = [
        pltpu.make_async_copy(grd_hbm, grd.at[pl.ds(pl.multiple_of(col * 128, 128), 128)], loc.at[0]),
        pltpu.make_async_copy(down_hbm.at[pl.ds(0, third)], down.at[pl.ds(0, third)], loc.at[1]),
        pltpu.make_async_copy(down_hbm.at[pl.ds(third, 2 * third)], down.at[pl.ds(third, 2 * third)], loc.at[2]),
        pltpu.make_async_copy(tok_hbm, tok.at[pl.ds(pl.multiple_of(col * 128, 128), 128)], loc.at[3]),
        pltpu.make_async_copy(up_hbm, up, loc.at[4]),
        pltpu.make_async_copy(relu_hbm, words, loc.at[5]),
        pltpu.make_async_copy(drop_hbm, dropped, loc.at[6]),
        pltpu.make_async_copy(bias_hbm, bias, loc.at[7]),
    ]
    for k in (0, 1, 5, 6):
        loads[k].start()

    barrier = pltpu.get_barrier_semaphore()
    for dev in everyone:
        pl.semaphore_signal(barrier, inc=1, device_id=dev, device_id_type=MESH)
    mirror = (y * 4 + x, col)

    @pl.when(x != y)
    def _():
        pl.semaphore_signal(barrier, inc=1, device_id=mirror, device_id_type=MESH)

    pl.semaphore_wait(barrier, len(everyone) + (x != y).astype(jnp.int32))

    def block_at(buf, zz, cc, lo=0, n=128):
        return buf.at[pl.ds(pl.multiple_of((zz * 2 + cc) * 128 + lo, 64), n)]

    def gather_copies(a, src, buf):
        s, r = ag_s.at[a], ag_r.at[a]
        mine = block_at(buf, z, c)
        below, above, opp = minus(z), plus(z), far(z)
        lower, upper = block_at(buf, z, c, 0, 64), block_at(buf, z, c, 64, 64)
        src_lower, src_upper = src.at[pl.ds(0, 64)], src.at[pl.ds(64, 64)]
        far_lower, far_upper = block_at(buf, opp, c, 0, 64), block_at(buf, opp, c, 64, 64)
        sends = [
            (src_lower, lower, zp),
            (src_upper, upper, zp),
            (src_upper, upper, zm),
            (src_lower, lower, zm),
            (src, mine, sib),
            (block_at(buf, below, c, 0, 64), block_at(buf, below, c, 0, 64), zp),
            (block_at(buf, above, c, 64, 64), block_at(buf, above, c, 64, 64), zm),
            (block_at(buf, below, c), block_at(buf, below, c), sib),
            (block_at(buf, above, c), block_at(buf, above, c), sib),
            (far_lower, far_lower, sib),
            (far_upper, far_upper, sib),
        ]
        o = 1 - c
        lands = [
            block_at(buf, below, c, 0, 64), block_at(buf, below, c, 64, 64),
            block_at(buf, above, c, 64, 64), block_at(buf, above, c, 0, 64),
            block_at(buf, z, o),
            far_lower, far_upper,
            block_at(buf, below, o), block_at(buf, above, o),
            block_at(buf, opp, o, 0, 64), block_at(buf, opp, o, 64, 64),
        ]

        def send(k):
            a, b, dev = sends[k]
            return remote(a, b, s, r.at[k], dev)

        def recv(k):
            return remote(lands[k], lands[k], s, r.at[k], zp)

        return send, recv

    def all_sent(a, buf):
        size = buf.at[pl.ds(0, 896)]
        remote(size, size, ag_s.at[a], ag_r.at[a, 0], zp).wait_send()

    def gather_0(a, src, buf):
        send, _ = gather_copies(a, src, buf)
        for k in (4, 0, 2, 1, 3):
            send(k).start()

    def gather_1(a, src, buf):
        send, recv = gather_copies(a, src, buf)
        for got, on in ((0, 5), (2, 6), (1, 7), (3, 8)):
            recv(got).wait_recv()
            send(on).start()

    def gather_2(a, src, buf):
        send, recv = gather_copies(a, src, buf)
        for got, on in ((5, 9), (6, 10)):
            recv(got).wait_recv()
            send(on).start()

    def gather_3(a, src, buf):
        send, recv = gather_copies(a, src, buf)
        for k in (4, 7, 8, 9, 10):
            recv(k).wait_recv()
        all_sent(a, buf)

    gather_0(0, grd_hbm, grd)
    for k in (2, 7):
        loads[k].start()

    swap = remote(words, swapped, sw_s, sw_r, mirror)
    loads[5].wait()
    loads[6].wait()
    words[...] = words[...] & dropped[...]

    @pl.when(x != y)
    def _():
        swap.start()

    @pl.when(x == y)
    def _():
        swapped[...] = words[...]

    def unpack(j):
        word = lax.broadcasted_iota(jnp.int32, (FB // 16, HALF), 0)
        unit = lax.broadcasted_iota(jnp.int32, (FB // 16, HALF), 1)
        bit = lax.broadcasted_iota(jnp.int32, (64, HALF), 1) % 16
        for f, ref in enumerate((swapped, words)):
            got = ref[...]
            low = (got & 255).astype(F32).astype(BF)
            high = (got >> 8).astype(F32).astype(BF)
            spread = (word == (j * WIDE + f * HALF + unit) // 16).astype(F32).astype(BF)
            lows = jnp.dot(low, spread, preferred_element_type=F32).astype(jnp.int32)
            highs = jnp.dot(high, spread, preferred_element_type=F32).astype(jnp.int32)
            picked = jnp.where(bit < 8, lows, highs)
            on = (picked >> (bit % 8)) & 1
            keep[:, pl.ds(pl.multiple_of(j * WIDE + f * HALF, HALF), HALF)] = on.astype(F32) * KEEP

    flavours = ((x, y, xp, xm, yp, ym, xf), (y, x, yp, ym, xp, xm, yf))

    def send_sem(p, n):
        first, length = SEND_RING[n]
        return ss.at[first + lax.rem(p, length)]

    def recv_sem(p, n):
        first, length = RECV_RING[n]
        return rs.at[first + lax.rem(p, length)]

    def forward_block(p, left, weight, q):
        w = lax.rem(p, RING)
        res = weight(left[pl.ds(pl.multiple_of(q * 256, 256), 256), :]).astype(BF)
        for f in range(2):
            for k in range(4):
                part[w, f, k, q] = res[k * 64 : (k + 1) * 64, f * HALF : (f + 1) * HALF]

    def early(q, first, end, pieces=1):
        top = q // 2

        def several(n, carry):
            for k in range(pieces):
                p = n * pieces + k
                rows = down[pl.ds(pl.multiple_of(p * WIDE, WIDE), WIDE), :]
                forward_block(p, grd, functools.partial(dot_nt, right=rows), q)
            for k in range(pieces):
                send_block(n * pieces + k)
            return carry

        def send_block(p):
            for f in range(2):
                d1 = flavours[f][0]
                pt, ra, rb = part.at[p, f], r1.at[p, f], r2.at[p, f]

                def along(off):
                    to = lax.rem(d1 + off, 4)
                    return to, ((to * 4 + y, col) if f == 0 else (x * 4 + to, col))

                _, dev = along(1 + 2 * top)
                remote(pt.at[far(d1), q], ra.at[top, q - 2 * top], send_sem(p, 0), recv_sem(p, 0), dev).start()
                to, dev = along(3 - 2 * top)
                remote(pt.at[to, q], rb.at[1 - top, q], send_sem(p, 0), recv_sem(p, 1), dev).start()

        lax.fori_loop(first // pieces, end // pieces, several, 0)

    loads[0].wait()
    loads[1].wait()

    def arrive(t, carry):
        send, recv = gather_copies(0, grd_hbm, grd)

        def forward_on(*pairs):
            for got, on in pairs:
                recv(got).wait_recv()
                send(on).start()

        @pl.when(t == 0)
        def _():
            recv(4).wait_recv()

        @pl.when(t == 1)
        def _():
            forward_on((0, 5), (2, 6))
            loads[2].wait()

        @pl.when(t == 2)
        def _():
            forward_on((1, 7), (3, 8))
            gather_0(1, tok_hbm, tok)
            loads[3].start()
            loads[4].start()
            recv(8).wait_recv()

        @pl.when(t == 3)
        def _():
            forward_on((5, 9), (6, 10))
            recv(7).wait_recv()

        @pl.when(t == 4)
        def _():
            for k in (9, 10):
                recv(k).wait_recv()

        u = (t * 4) // 5
        first = (t == 1).astype(jnp.int32) * (EARLY // 2)
        end = EARLY + (t == 1).astype(jnp.int32) * (NJ - EARLY) - (t == 0).astype(jnp.int32) * (EARLY - EARLY // 2)
        early(lax.rem(z + u + u // 2 - 2 * (u // 3), 4), first, end, 2)
        return carry

    lax.fori_loop(0, 5, arrive, 0)
    all_sent(0, grd)
    loads[7].wait()

    def piece(p, f):
        d1, d2, p1, m1, p2, m2, f1 = flavours[f]
        w, v = lax.rem(p, RING), lax.rem(p, HELD)
        pt, sm, g = part.at[w, f], summed.at[w, f], full.at[v, f]
        ra, rb, ta, tb = r1.at[w, f], r2.at[w, f], t1.at[w, f], t2.at[w, f]
        lo, hi = pl.ds(0, 2), pl.ds(2, 2)
        lo3, hi3 = pl.ds(0, 32), pl.ds(32, 32)
        n1, b1, o1 = plus(d1), minus(d1), far(d1)
        n2, b2, o2 = plus(d2), minus(d2), far(d2)
        sends = (
            (pt.at[o1, lo], ra.at[0], p1),
            (pt.at[o1, hi], ra.at[1], m1),
            (pt.at[n1, hi], rb.at[0, hi], p1),
            (pt.at[b1, lo], rb.at[1, lo], m1),
            (pt.at[n1, lo], rb.at[0, lo], p1),
            (pt.at[b1, hi], rb.at[1, hi], m1),
            (sm.at[o2, lo3], ta.at[0], p2),
            (sm.at[o2, hi3], ta.at[1], m2),
            (sm.at[n2, hi3], tb.at[0, hi3], p2),
            (sm.at[b2, lo3], tb.at[1, lo3], m2),
            (sm.at[n2, lo3], tb.at[0, lo3], p2),
            (sm.at[b2, hi3], tb.at[1, hi3], m2),
            (g.at[d1, d2], g.at[d1, d2], p2),
            (g.at[d1, d2], g.at[d1, d2], m2),
            (g.at[d1, b2, lo3], g.at[d1, b2, lo3], p2),
            (g.at[d1, n2, hi3], g.at[d1, n2, hi3], m2),
            (g.at[d1], g.at[d1], p1),
            (g.at[d1], g.at[d1], m1),
            (g.at[b1, lo], g.at[b1, lo], p1),
            (g.at[n1, hi], g.at[n1, hi], m1),
            (g.at[d1], g.at[d1], f1),
        )

        def start(*ks):
            for k in ks:
                a, b, dev = sends[k]
                remote(a, b, send_sem(p, min(k // 6, 2)), recv_sem(p, GROUP[k]), dev).start()

        return start

    def landed(p, n):
        w, v = lax.rem(p, RING), lax.rem(p, HELD)
        g = full.at[v, 0]
        size = (r1.at[w], r2.at[w], t1.at[w], t2.at[w], g.at[0], g.at[0, pl.ds(0, 2)], g, g.at[pl.ds(0, 2)])[n]
        remote(size, size, send_sem(p, 0), recv_sem(p, n), xp).wait_recv()

    def sent(p, n):
        size = grd.at[pl.ds(0, (256, 64, 320)[n])]
        remote(size, size, send_sem(p, n), recv_sem(p, 0), xp).wait_send()

    def when_piece(i, lag):
        p = i - lag
        return p, (p >= 0) & (p < NP)

    def stage_a(p):
        @pl.when(p < NJ)
        def _():
            def other(n, carry):
                early(lax.rem(z + n, 4), p, p + 1)
                return carry

            lax.fori_loop(1, 4, other, 0)

        @pl.when(p >= NJ)
        def _():
            lanes = up[:, pl.ds(pl.multiple_of((p - NJ) * WIDE, WIDE), WIDE)]
            for q in range(4):
                forward_block(p, tok, lambda left: jnp.dot(left, lanes, preferred_element_type=F32), q)
            for f in range(2):
                start = piece(p, f)
                start(0, 1, 2, 3)

    def stage_b(p):
        w = lax.rem(p, RING)
        landed(p, 0)
        for f in range(2):
            d1 = flavours[f][0]
            start = piece(p, f)
            n1, b1 = plus(d1), minus(d1)
            part[w, f, n1, 0:2] = (part[w, f, n1, 0:2].astype(F32) + r1[w, f, 0].astype(F32)).astype(BF)
            part[w, f, b1, 2:4] = (part[w, f, b1, 2:4].astype(F32) + r1[w, f, 1].astype(F32)).astype(BF)
            start(4, 5)

    def stage_c(p):
        w = lax.rem(p, RING)
        landed(p, 1)
        for f in range(2):
            d1 = flavours[f][0]
            start = piece(p, f)
            total = part[w, f, d1].astype(F32) + r2[w, f, 0].astype(F32) + r2[w, f, 1].astype(F32)
            summed[w, f] = total.astype(BF)
            start(6, 7, 8, 9)

    def stage_d(p):
        w = lax.rem(p, RING)
        landed(p, 2)
        sent(p, 0)
        for f in range(2):
            d2 = flavours[f][1]
            start = piece(p, f)
            n2, b2 = plus(d2), minus(d2)
            summed[w, f, n2, 0:32] = (summed[w, f, n2, 0:32].astype(F32) + t1[w, f, 0].astype(F32)).astype(BF)
            summed[w, f, b2, 32:64] = (summed[w, f, b2, 32:64].astype(F32) + t1[w, f, 1].astype(F32)).astype(BF)
            start(10, 11)

    def stage_e(p):
        w, v = lax.rem(p, RING), lax.rem(p, HELD)
        landed(p, 3)
        j = lax.rem(p, NJ)
        on_pre = (p >= NJ).astype(F32)
        for f in range(2):
            d1, d2 = flavours[f][:2]
            start = piece(p, f)
            total = summed[w, f, d2].astype(F32) + t2[w, f, 0].astype(F32) + t2[w, f, 1].astype(F32)
            lanes = pl.ds(pl.multiple_of(j * WIDE + f * HALF, HALF), HALF)
            total = total + bias[0:1, lanes] * on_pre
            full[v, f, d1, d2] = (keep[:, lanes] * total).astype(BF)
            start(12, 13)

    def stage_f(p):
        landed(p, 4)
        sent(p, 1)
        for f in range(2):
            start = piece(p, f)
            start(14, 15)

    def stage_g(p):
        landed(p, 5)
        for f in range(2):
            start = piece(p, f)
            start(16, 17)
            pl.when(p >= NP - LATE)(functools.partial(start, 20))

    def stage_h(p):
        landed(p, 6)
        for f in range(2):
            start = piece(p, f)
            pl.when(p < NP - LATE)(functools.partial(start, 18, 19))

    def collect(p, ref):
        w = lax.rem(p, HELD)
        landed(p, 7)
        for f in range(2):
            for q in range(4):
                for k in range(4):
                    ref[(q * 4 + k) * 64 : (q * 4 + k + 1) * 64, f * HALF : (f + 1) * HALF] = full[w, f, k, q]

    def stage_m(p):
        collect(p, cols)

        @pl.when(p < NJ)
        def _():
            j = p
            lanes = pl.ds(pl.multiple_of(j * WIDE, WIDE), WIDE)

            for q in range(3):
                res = jnp.dot(tok_t[q * 256 : (q + 1) * 256, :], cols[...], preferred_element_type=F32)
                gu_out[q * 256 : (q + 1) * 256, lanes] = (res * SCALE).astype(BF)
            gb_out[0:1, lanes] = jnp.sum(cols[...].astype(F32), axis=0, keepdims=True) * SCALE
            for q in range(4):
                acc[q * 256 : (q + 1) * 256, :] += dot_nt(cols[q * 256 : (q + 1) * 256, :], up[:, lanes])

        @pl.when(p >= NJ)
        def _():
            j = p - NJ

            res = lax.dot_general(cols[...], grd[...], (((0,), (0,)), ((), ())), preferred_element_type=F32)
            gd_out[pl.ds(pl.multiple_of(j * WIDE, WIDE), WIDE), :] = (res * SCALE).astype(BF)

        sent(p, 2)

    def gt_copies():
        s, r = gt_s, gt_r
        mine = gtp.at[c]
        above, below, opp = plus(z), minus(z), far(z)
        lo, hi = pl.ds(0, 64), pl.ds(64, 64)
        sends = [
            (gtp.at[1 - c], gtr, sib),
            (mine.at[opp, lo], z1.at[0], zp),
            (mine.at[opp, hi], z1.at[1], zm),
            (mine.at[above, hi], z2.at[0, hi], zp),
            (mine.at[below, lo], z2.at[1, lo], zm),
            (mine.at[above, lo], z2.at[0, lo], zp),
            (mine.at[below, hi], z2.at[1, hi], zm),
        ]

        def send(k):
            a, b, dev = sends[k]
            return remote(a, b, s, r.at[k], dev)

        return send

    def gt_0():
        for q in range(8):
            gtp[q % 2, q // 2] = acc[q * 128 : (q + 1) * 128, :].astype(BF)
        gt_copies()(0).start()

    def gt_1():
        send = gt_copies()
        send(0).wait_recv()
        for q in range(4):
            gtp[c, q] = (gtp[c, q].astype(F32) + gtr[q].astype(F32)).astype(BF)
        for k in (1, 2, 3, 4):
            send(k).start()

    def gt_2():
        send = gt_copies()
        send(1).wait_recv()
        send(2).wait_recv()
        above, below = plus(z), minus(z)
        gtp[c, above, 0:64] = (gtp[c, above, 0:64].astype(F32) + z1[0].astype(F32)).astype(BF)
        gtp[c, below, 64:128] = (gtp[c, below, 64:128].astype(F32) + z1[1].astype(F32)).astype(BF)
        send(5).start()
        send(6).start()

    def gt_3():
        send = gt_copies()
        for k in (3, 4, 5, 6):
            send(k).wait_recv()
        gt_out[...] = (gtp[c, z].astype(F32) + z2[0].astype(F32) + z2[1].astype(F32)).astype(BF)
        size = tok.at[pl.ds(0, 896)]
        remote(size, size, gt_s, gt_r.at[0], sib).wait_send()

    def step(i, carry):
        for fn, lag in (
            (stage_h, LAG_H), (stage_g, LAG_G), (stage_f, LAG_F), (stage_e, LAG_E),
            (stage_d, LAG_D), (stage_c, LAG_C), (stage_b, LAG_B), (stage_a, LAG_A), (stage_m, LAG_M),
        ):
            p, on = when_piece(i, lag)
            on = on & (p >= EARLY) if fn is stage_a else on
            pl.when(on)(functools.partial(fn, p))

        def at(n):
            return pl.when(i == n)

        @pl.when((i == 0) & (x != y))
        def _():
            swap.wait()

        pl.when((i >= 5) & (i < NJ + 5))(functools.partial(unpack, i - 5))

        @at(0)
        def _():
            gather_1(1, tok_hbm, tok)

        @at(2)
        def _():
            gather_2(1, tok_hbm, tok)
            loads[3].wait()
            loads[4].wait()

        @at(3)
        def _():
            gather_3(1, tok_hbm, tok)

        @at(12)
        def _():
            acc[...] = jnp.zeros_like(acc)
            for q in range(8):
                tok_t[:, q * 128 : (q + 1) * 128] = tok[q * 128 : (q + 1) * 128, :].T

        last = LAG_M + NJ - 1
        at(last)(gt_0)
        at(last + 2)(gt_1)
        at(last + 4)(gt_2)
        at(last + 7)(gt_3)
        return carry

    lax.fori_loop(0, NP + LAG_H, step, 0)
    for k in range(LATE):
        collect(NP - LATE + k, late.at[k])
        sent(NP - LATE + k, 2)


def flush(gt, gu, gd, gb, late, grd, gt_out, gu_out, gd_out, gb_out, rows, sem):
    done = FB - LATE * WIDE
    copies = [pltpu.make_async_copy(gt, gt_out, sem.at[0]), pltpu.make_async_copy(gb, gb_out, sem.at[1])]
    for q in range(4):
        part = pl.ds(q * DB // 4, DB // 4)
        copies.append(pltpu.make_async_copy(gu.at[part], gu_out.at[part], sem.at[2 + q]))
        part = pl.ds(q * done // 4, done // 4)
        copies.append(pltpu.make_async_copy(gd.at[part], gd_out.at[part], sem.at[6 + q]))
    for cp in copies:
        cp.start()
    for k in range(LATE):
        res = lax.dot_general(late[k], grd[...], (((0,), (0,)), ((), ())), preferred_element_type=F32)
        rows[k] = (res * SCALE).astype(BF)
        cp = pltpu.make_async_copy(rows.at[k], gd_out.at[pl.ds(done + k * WIDE, WIDE)], sem.at[10 + k])
        cp.start()
        copies.append(cp)
    for cp in copies:
        cp.wait()


def body(tokens, grad_out, up_weight, down_weight, up_bias, relu_bits, drop_bits):
    hbm = pl.BlockSpec(memory_space=pl.ANY)
    vmem = pl.BlockSpec(memory_space=pltpu.VMEM)
    dma = pltpu.SemaphoreType.DMA
    shapes = (((128, DB), BF), ((DB, FB), BF), ((FB, DB), BF), ((1, FB), F32))
    kept = (((LATE, TOK, WIDE), BF), ((TOK, DB), BF))
    held = pl.pallas_call(
        kernel,
        out_shape=tuple(pltpu.VMEM(shape, dtype) for shape, dtype in shapes + kept),
        in_specs=[hbm] * 7,
        out_specs=(vmem,) * 6,
        scratch_shapes=[
            pltpu.VMEM((TOK, DB), BF),
            pltpu.VMEM((DB, TOK), BF),
            pltpu.VMEM((DB, FB), BF),
            pltpu.VMEM((FB, DB), BF),
            pltpu.VMEM((64, FB), F32),
            pltpu.VMEM((TOK, DB), F32),
            pltpu.VMEM((TOK, WIDE), BF),
            pltpu.VMEM((RING, 2, 4, 4, 64, HALF), BF),
            pltpu.VMEM((RING, 2, 2, 2, 64, HALF), BF),
            pltpu.VMEM((RING, 2, 2, 4, 64, HALF), BF),
            pltpu.VMEM((RING, 2, 4, 64, HALF), BF),
            pltpu.VMEM((RING, 2, 2, 32, HALF), BF),
            pltpu.VMEM((RING, 2, 2, 64, HALF), BF),
            pltpu.VMEM((HELD, 2, 4, 4, 64, HALF), BF),
            pltpu.VMEM((2, 4, 128, DB), BF),
            pltpu.VMEM((4, 128, DB), BF),
            pltpu.VMEM((2, 64, DB), BF),
            pltpu.VMEM((2, 128, DB), BF),
            pltpu.VMEM((64, FB // 16), jnp.int32),
            pltpu.VMEM((64, FB // 16), jnp.int32),
            pltpu.VMEM((64, FB // 16), jnp.int32),
            pltpu.VMEM((1, FB), F32),
            dma((N_SEND,)),
            dma((N_RECV,)),
            dma((2,)),
            dma((2, 11)),
            dma,
            dma((7,)),
            dma,
            dma,
            dma((8,)),
        ],
        compiler_params=pltpu.CompilerParams(
            collective_id=0, has_side_effects=True, vmem_limit_bytes=48 * 2**20
        ),
        cost_estimate=pl.CostEstimate(
            flops=10 * TOK * DB * FB, bytes_accessed=10 * DB * FB, transcendentals=0
        ),
        name="fused",
    )(tokens, grad_out, up_weight, down_weight, up_bias.reshape(1, FB), relu_bits, drop_bits)
    gt, gu, gd, gb = pl.pallas_call(
        flush,
        out_shape=tuple(jax.ShapeDtypeStruct(shape, dtype) for shape, dtype in shapes),
        in_specs=[vmem] * 6,
        out_specs=(hbm,) * 4,
        scratch_shapes=[pltpu.VMEM((LATE, WIDE, DB), BF), dma((10 + LATE,))],
        compiler_params=pltpu.CompilerParams(vmem_limit_bytes=6 * 2**20),
        name="flush",
    )(*held)
    return gt, gu, gd, gb.reshape(FB)


def solution(mesh):
    return jax.shard_map(
        body,
        mesh=mesh,
        in_specs=(
            P("col", "row"), P("col", "row"), P("row", "col"), P("col", "row"),
            P("col"), P("row", "col"), P("row", "col"),
        ),
        out_specs=(P("col", "row"), P("row", "col"), P("col", "row"), P("col")),
        check_vma=False,
    )
```
